32 devices in a mesh: groups: 2 (over y), row: 4 (over z), col: 4 (over x, core).
Axes of the slice: x: 2, y: 2, z: 4, core: 2. Of those that a mesh axis runs over, the one named last changes fastest.
Arguments:
- pair: bfloat16 [128, 64, 128], P(('groups', 'row'), 'col'), parts along dimension 0, may hold values from -6 to 6
- pair_cotangent: bfloat16 [128, 64, 128], P(('groups', 'row'), 'col'), parts along dimension 0, may hold values from -6 to 6
- edge_weights: bfloat16 [2, 128, 640], replicated, may hold values from -0.5 to 0.5
- out_weights: bfloat16 [2, 128, 128], replicated, may hold values from -0.5 to 0.5
- norm_gains: float32 [2, 2, 128], replicated, may hold values from 0.1 to 1.9
- norm_shifts: float32 [2, 2, 128], replicated, may hold values from -3 to 3
Outputs:
- pair_grad: bfloat16 [128, 64, 128], P(('groups', 'row'), 'col'), parts along dimension 0
- edge_grads: bfloat16 [4, 128, 64, 128], P(None, ('groups', 'row'), 'col'), parts along dimension 1
The draws below stay inside these ranges and needn't reach their ends.
There are 2 independent parts, one for each index of `groups`. The reference program is written for one: setup_inputs(seed, part) draws one part's arguments, and reference() takes and returns one part's arrays. A program takes and returns all parts, laid end to end along the dimension named above; an argument that names none is the same for every part. Nothing has to cross between parts.
All inputs are finite; a program needn't handle non-finite values.
Results may differ from the reference program's by a relative error of at most 0.012.
Values may be sent and summed in bfloat16 or wider, within the bound.
A program may use at most 128 MiB of HBM per device.

```python
import jax
import jax.numpy as jnp
from jax import lax

PAIR = 128
EDGE = 128
RESIDUES = 64


def block_levels(key, shape, cuts, smallest, high):
    loudness, own = 1.0, jax.random.fold_in(key, 6)
    for position, shards_of in cuts:
        draws = jnp.exp(jax.random.uniform(jax.random.fold_in(own, position), (shards_of,), jnp.float32, smallest / len(cuts), high / len(cuts)))
        loudness = loudness * jnp.repeat(draws, shape[position] // shards_of).reshape([-1 if axis == position else 1 for axis in range(len(shape))])
    return loudness


def scatter_about(key, extent, scale, limit, cuts=(), kind=jnp.bfloat16):
    level = block_levels(key, extent, cuts, -0.22, 0.18) if cuts else 1.0
    drawn = jax.random.normal(key, extent, jnp.float32) * scale * level
    return jnp.minimum(jnp.maximum(drawn, -limit), limit).astype(kind)


def setup_inputs(seed: int = 0, part: int = 0) -> dict:
    arg_keys = jax.random.split(jax.random.key(seed), 7)
    part_keys = jax.random.split(jax.random.fold_in(arg_keys[6], part), 7)
    pair = scatter_about(part_keys[0], (RESIDUES, RESIDUES, PAIR), 1.0, 6.0, ((0, 4), (1, 4)))
    pair_cotangent = scatter_about(part_keys[1], (RESIDUES, RESIDUES, PAIR), 1.0, 6.0, ((0, 4), (1, 4)))
    edge_weights = scatter_about(arg_keys[2], (2, PAIR, 5 * EDGE), PAIR ** -0.5, 0.5)
    out_weights = scatter_about(arg_keys[3], (2, EDGE, PAIR), EDGE ** -0.5, 0.5)
    norm_gains = jnp.clip(1.0 + 0.18 * jax.random.normal(arg_keys[4], (2, 2, PAIR), jnp.float32), 0.1, 1.9)
    norm_shifts = scatter_about(arg_keys[5], (2, 2, PAIR), 0.5, 3.0, (), jnp.float32)
    return {"pair": pair, "pair_cotangent": pair_cotangent, "edge_weights": edge_weights, "out_weights": out_weights, "norm_gains": norm_gains, "norm_shifts": norm_shifts}


EPSILON = 1e-05

def rounded(values):
    return lax.optimization_barrier(values.astype(jnp.bfloat16)).astype(jnp.float32)

def product_of(form, left, right):
    return jnp.einsum(form, left.astype(jnp.float32), right.astype(jnp.float32), precision=lax.Precision.HIGHEST)

def layer_norm(inputs, norm_gain, norm_shift):
    centre = lax.optimization_barrier(jnp.mean(inputs, axis=-1, keepdims=True))
    centred = inputs - centre
    inverse = lax.rsqrt(lax.optimization_barrier(jnp.mean(centred * centred, axis=-1, keepdims=True)) + EPSILON)
    standard = centred * inverse
    return (standard, inverse, standard * norm_gain + norm_shift)

def norm_backward(upstream, standard, inverse, norm_gain):
    scaled = upstream * norm_gain
    mean_grad = lax.optimization_barrier(jnp.mean(scaled, axis=-1, keepdims=True))
    second = lax.optimization_barrier(jnp.mean(scaled * standard, axis=-1, keepdims=True))
    return (scaled - mean_grad - standard * second) * inverse

def edges_forward(inputs, weights, norm_gain, norm_shift):
    standard, inverse, normed = layer_norm(inputs, norm_gain, norm_shift)
    projected = product_of('ijc,cd->ijd', rounded(normed), weights)
    width = weights.shape[1] // 5
    value_left = projected[..., :width]
    sigma_left = jax.nn.sigmoid(projected[..., width:2 * width])
    value_right = projected[..., 2 * width:3 * width]
    sigma_right = jax.nn.sigmoid(projected[..., 3 * width:4 * width])
    out_gate = jax.nn.sigmoid(projected[..., 4 * width:])
    left_edge = rounded(sigma_left * value_left)
    right_edge = rounded(sigma_right * value_right)
    saved = (standard, inverse, value_left, sigma_left, value_right, sigma_right, out_gate)
    return (left_edge, right_edge, saved)

def output_forward(product, out_weight, norm_gain, norm_shift):
    standard, inverse, normed = layer_norm(product, norm_gain, norm_shift)
    hidden_out = product_of('ijd,dc->ijc', rounded(normed), out_weight)
    return (hidden_out, standard, inverse)

def output_backward(upstream, out_weight, norm_gain, out_gate, stats):
    hidden_out, standard, inverse = stats
    grad_hidden = rounded(upstream * out_gate)
    gate_term = upstream * hidden_out * out_gate * (1.0 - out_gate)
    grad_normed = product_of('ijc,dc->ijd', grad_hidden, out_weight)
    grad_product = rounded(norm_backward(grad_normed, standard, inverse, norm_gain))
    return (grad_product, gate_term)

def edges_backward(grad_left, grad_right, gate_term, weights, norm_gain, saved):
    standard, inverse, value_left, sigma_left, value_right, sigma_right, out_gate = saved
    pieces = jnp.concatenate([grad_left * sigma_left, grad_left * value_left * sigma_left * (1.0 - sigma_left), grad_right * sigma_right, grad_right * value_right * sigma_right * (1.0 - sigma_right), gate_term], axis=-1)
    grad_normed = product_of('ijd,cd->ijc', rounded(pieces), weights)
    return norm_backward(grad_normed, standard, inverse, norm_gain)

def reference(pair, pair_cotangent, edge_weights, out_weights, norm_gains, norm_shifts):
    pair_float = pair.astype(jnp.float32)
    left_out, right_out, saved_out = edges_forward(pair_float, edge_weights[0], norm_gains[0, 0], norm_shifts[0, 0])
    product_out = product_of('ikc,jkc->ijc', left_out, right_out)
    stats_out = output_forward(product_out, out_weights[0], norm_gains[0, 1], norm_shifts[0, 1])
    middle = rounded(pair_float + saved_out[6] * stats_out[0])
    left_in, right_in, saved_in = edges_forward(middle, edge_weights[1], norm_gains[1, 0], norm_shifts[1, 0])
    product_in = product_of('kic,kjc->ijc', left_in, right_in)
    stats_in = output_forward(product_in, out_weights[1], norm_gains[1, 1], norm_shifts[1, 1])
    upstream = pair_cotangent.astype(jnp.float32)
    grad_product_in, gate_in = output_backward(upstream, out_weights[1], norm_gains[1, 1], saved_in[6], stats_in)
    grad_left_in = product_of('ijc,kjc->kic', grad_product_in, right_in)
    grad_right_in = product_of('kic,ijc->kjc', left_in, grad_product_in)
    grad_middle = upstream + edges_backward(grad_left_in, grad_right_in, gate_in, edge_weights[1], norm_gains[1, 0], saved_in)
    grad_product_out, gate_outer = output_backward(grad_middle, out_weights[0], norm_gains[0, 1], saved_out[6], stats_out)
    grad_left_out = product_of('ijc,jkc->ikc', grad_product_out, right_out)
    grad_right_out = product_of('ijc,ikc->jkc', grad_product_out, left_out)
    pair_grad = grad_middle + edges_backward(grad_left_out, grad_right_out, gate_outer, edge_weights[0], norm_gains[0, 0], saved_out)
    edge_grads = jnp.stack([grad_left_out, grad_right_out, grad_left_in, grad_right_in])
    return (pair_grad.astype(jnp.bfloat16), edge_grads.astype(jnp.bfloat16))
```

```python
import functools

import jax
import jax.numpy as jnp
from jax import lax
from jax.experimental import pallas as pl
from jax.experimental.pallas import tpu as pltpu
from jax.sharding import PartitionSpec as P

EPSILON = 1e-05


def product_of(form, left, right):
    return jnp.einsum(form, left, right, preferred_element_type=jnp.float32)


def layer_norm(inputs, norm_gain, norm_shift):
    centre = jnp.mean(inputs, axis=-1, keepdims=True)
    centred = inputs - centre
    inverse = lax.rsqrt(jnp.mean(centred * centred, axis=-1, keepdims=True) + EPSILON)
    standard = centred * inverse
    return (standard, inverse, standard * norm_gain + norm_shift)


def norm_backward(upstream, standard, inverse, norm_gain):
    scaled = upstream * norm_gain
    mean_grad = jnp.mean(scaled, axis=-1, keepdims=True)
    second = jnp.mean(scaled * standard, axis=-1, keepdims=True)
    return (scaled - mean_grad - standard * second) * inverse


def edges_forward(inputs, weights, norm_gain, norm_shift):
    standard, inverse, normed = layer_norm(inputs, norm_gain, norm_shift)
    projected = product_of("ijc,cd->ijd", normed.astype(jnp.bfloat16), weights)
    width = weights.shape[1] // 5
    value_left = projected[..., :width]
    sigma_left = jax.nn.sigmoid(projected[..., width : 2 * width])
    value_right = projected[..., 2 * width : 3 * width]
    sigma_right = jax.nn.sigmoid(projected[..., 3 * width : 4 * width])
    out_gate = jax.nn.sigmoid(projected[..., 4 * width :])
    left_edge = (sigma_left * value_left).astype(jnp.bfloat16)
    right_edge = (sigma_right * value_right).astype(jnp.bfloat16)
    saved = (standard, inverse, value_left, sigma_left, value_right, sigma_right, out_gate)
    return (left_edge, right_edge, saved)


def output_forward(product, out_weight, norm_gain, norm_shift):
    standard, inverse, normed = layer_norm(product, norm_gain, norm_shift)
    hidden_out = product_of("ijd,dc->ijc", normed.astype(jnp.bfloat16), out_weight)
    return (hidden_out, standard, inverse)


def output_backward(upstream, out_weight, norm_gain, out_gate, stats):
    hidden_out, standard, inverse = stats
    grad_hidden = (upstream * out_gate).astype(jnp.bfloat16)
    gate_term = upstream * hidden_out * out_gate * (1.0 - out_gate)
    grad_normed = product_of("ijc,dc->ijd", grad_hidden, out_weight)
    grad_product = norm_backward(grad_normed, standard, inverse, norm_gain).astype(jnp.bfloat16)
    return (grad_product, gate_term)


def edges_backward(grad_left, grad_right, gate_term, weights, norm_gain, saved):
    standard, inverse, value_left, sigma_left, value_right, sigma_right, out_gate = saved
    pieces = jnp.concatenate(
        [
            grad_left * sigma_left,
            grad_left * value_left * sigma_left * (1.0 - sigma_left),
            grad_right * sigma_right,
            grad_right * value_right * sigma_right * (1.0 - sigma_right),
            gate_term,
        ],
        axis=-1,
    )
    grad_normed = product_of("ijd,cd->ijc", pieces.astype(jnp.bfloat16), weights)
    return norm_backward(grad_normed, standard, inverse, norm_gain)


def row_strip(tile):
    return lax.all_gather(tile, "col", axis=1, tiled=True)


def column_strip(tile):
    return lax.all_gather(tile, "row", axis=0, tiled=True)


def shuffle_rows(tile):
    return lax.all_to_all(tile, "row", split_axis=1, concat_axis=0, tiled=True)


def shuffle_columns(tile):
    return lax.all_to_all(tile, "col", split_axis=0, concat_axis=1, tiled=True)


def transposed_columns(tile):
    row_devices = lax.axis_size("row")
    column_devices = lax.axis_size("col")
    moved = shuffle_columns(shuffle_rows(tile))
    gathered = column_strip(jnp.swapaxes(moved, 0, 1))
    total = gathered.shape[0]
    block = total // (row_devices * column_devices)
    gathered = gathered.reshape(
        row_devices, column_devices, block, gathered.shape[1], gathered.shape[2]
    )
    return jnp.swapaxes(gathered, 0, 1).reshape(total, gathered.shape[3], gathered.shape[4])


def transposed_rows(tile):
    row_devices = lax.axis_size("row")
    column_devices = lax.axis_size("col")
    moved = shuffle_rows(shuffle_columns(tile))
    gathered = row_strip(jnp.swapaxes(moved, 0, 1))
    total = gathered.shape[1]
    block = total // (row_devices * column_devices)
    gathered = gathered.reshape(
        gathered.shape[0], column_devices, row_devices, block, gathered.shape[2]
    )
    return jnp.swapaxes(gathered, 1, 2).reshape(gathered.shape[0], total, gathered.shape[4])


def gathered_body(pair, pair_cotangent, edge_weights, out_weights, norm_gains, norm_shifts):
    pair_float = pair.astype(jnp.float32)
    left_out, right_out, saved_out = edges_forward(
        pair_float, edge_weights[0], norm_gains[0, 0], norm_shifts[0, 0]
    )
    strip_right = column_strip(right_out)
    product_out = product_of("ikc,kjc->ijc", row_strip(left_out), transposed_columns(right_out))
    stats_out = output_forward(product_out, out_weights[0], norm_gains[0, 1], norm_shifts[0, 1])
    middle = (pair_float + saved_out[6] * stats_out[0]).astype(jnp.bfloat16)
    left_in, right_in, saved_in = edges_forward(
        middle.astype(jnp.float32), edge_weights[1], norm_gains[1, 0], norm_shifts[1, 0]
    )
    product_in = product_of("ikc,kjc->ijc", transposed_rows(left_in), column_strip(right_in))
    stats_in = output_forward(product_in, out_weights[1], norm_gains[1, 1], norm_shifts[1, 1])
    upstream = pair_cotangent.astype(jnp.float32)
    grad_product_in, gate_in = output_backward(
        upstream, out_weights[1], norm_gains[1, 1], saved_in[6], stats_in
    )
    grad_left_in = product_of(
        "kjc,jic->kic", row_strip(right_in), transposed_columns(grad_product_in)
    )
    grad_right_in = product_of("kic,ijc->kjc", row_strip(left_in), column_strip(grad_product_in))
    grad_middle = upstream + edges_backward(
        grad_left_in, grad_right_in, gate_in, edge_weights[1], norm_gains[1, 0], saved_in
    )
    grad_product_out, gate_outer = output_backward(
        grad_middle, out_weights[0], norm_gains[0, 1], saved_out[6], stats_out
    )
    grad_left_out = product_of("ijc,jkc->ikc", row_strip(grad_product_out), strip_right)
    grad_right_out = product_of(
        "jic,ikc->jkc", transposed_rows(grad_product_out), column_strip(left_out)
    )
    pair_grad = grad_middle + edges_backward(
        grad_left_out, grad_right_out, gate_outer, edge_weights[0], norm_gains[0, 0], saved_out
    )
    edge_grads = jnp.stack([grad_left_out, grad_right_out, grad_left_in, grad_right_in])
    return (pair_grad.astype(jnp.bfloat16), edge_grads.astype(jnp.bfloat16))


MESH = pl.DeviceIdType.MESH
LEFT_OUT, RIGHT_OUT, LEFT_IN, RIGHT_IN = range(4)
STANDARD, VALUE_LEFT, SIGMA_LEFT, VALUE_RIGHT, SIGMA_RIGHT, GATE, HIDDEN, CENTRED = range(8)


def matmul(left, right):
    return jnp.dot(left, right, preferred_element_type=jnp.float32)


def matmul_transposed(left, right):
    return lax.dot_general(
        left, right, (((1,), (1,)), ((), ())), preferred_element_type=jnp.float32
    )


def kernel(
    parts,
    side,
    pair_ref,
    cotangent_ref,
    edge_weights_ref,
    out_weights_ref,
    gains_ref,
    shifts_ref,
    pair_grad_ref,
    edge_grads_ref,
    own,
    strips,
    partials,
    sums,
    wide,
    saved,
    inverses,
    projected,
    work,
    grads,
    middle,
    upstream,
    pieces,
    strip_send,
    strip_recv,
    sum_send,
    sum_recv,
):
    row = lax.axis_index("row")
    col = lax.axis_index("col")
    area = side * side
    diagonal = row == col
    chunk = min(area, 64)

    def turned(index, step):
        return lax.rem(index + step, parts)

    barrier = pltpu.get_barrier_semaphore()
    me = row * parts + col
    others = parts * parts - 1

    def greet(step, carry):
        other = lax.rem(me + step, parts * parts)
        pl.semaphore_signal(
            barrier,
            inc=1,
            device_id={"row": other // parts, "col": lax.rem(other, parts)},
            device_id_type=MESH,
        )
        return carry

    lax.fori_loop(1, others + 1, greet, 0)

    def in_chunks(step):
        def run(index, carry):
            step(pl.ds(pl.multiple_of(index * chunk, chunk), chunk))
            return carry

        lax.fori_loop(0, area // chunk, run, 0)

    def remote(source, target, send_sem, recv_sem, device):
        return pltpu.make_async_remote_copy(
            src_ref=source,
            dst_ref=target,
            send_sem=send_sem,
            recv_sem=recv_sem,
            device_id={"row": device[0], "col": device[1]},
            device_id_type=MESH,
        )

    def route(kind, step):
        if kind == "row":
            return (row, turned(col, step)), turned(col, step), col
        if kind == "col":
            return (turned(row, step), col), turned(row, step), row
        if kind == "to_col":
            return (turned(row, step), row), turned(row, step), col
        return (col, turned(col, step)), turned(col, step), row

    def ship(kind, step, source, buffer, which, send_sems, recv_sems):
        device, _, slot = route(kind, step)
        copy = remote(
            source,
            buffer.at[which, slot],
            send_sems.at[which, step],
            recv_sems.at[which, slot],
            device,
        )
        if step > 0:
            copy.start()
            return
        local = pltpu.make_async_copy(source, buffer.at[which, slot], recv_sems.at[which, slot])
        if kind in ("row", "col"):
            local.start()
        else:
            pl.when(diagonal)(local.start)
            pl.when(jnp.logical_not(diagonal))(copy.start)

    def shipped(kind, step, source, buffer, which, send_sems, recv_sems):
        device, _, slot = route(kind, step)
        copy = remote(
            source,
            buffer.at[which, slot],
            send_sems.at[which, step],
            recv_sems.at[which, slot],
            device,
        )
        if step > 0:
            copy.wait_send()
        elif kind not in ("row", "col"):
            pl.when(jnp.logical_not(diagonal))(copy.wait_send)

    def landed(buffer, which, slot, send_sems, recv_sems):
        remote(
            buffer.at[which, slot],
            buffer.at[which, slot],
            send_sems.at[which, 0],
            recv_sems.at[which, slot],
            (row, col),
        ).wait_recv()

    def project(update, source, cast):
        gain = gains_ref[update, 0:1, :]
        shift = shifts_ref[update, 0:1, :]

        def norm_step(rows):
            inputs = source[rows, :].astype(jnp.float32)
            standard, inverse, normed = layer_norm(inputs, gain, shift)
            saved[update, STANDARD, rows, :] = standard
            inverses[update, 0, rows, :] = jnp.broadcast_to(inverse, standard.shape)
            cast[rows, :] = normed.astype(jnp.bfloat16)

        in_chunks(norm_step)
        projected[...] = matmul(cast[...], edge_weights_ref[update])

        def gate_step(rows):
            width = gain.shape[1]
            value_left = projected[rows, 0:width]
            sigma_left = jax.nn.sigmoid(projected[rows, width : 2 * width])
            value_right = projected[rows, 2 * width : 3 * width]
            sigma_right = jax.nn.sigmoid(projected[rows, 3 * width : 4 * width])
            own[2 * update, rows, :] = (sigma_left * value_left).astype(jnp.bfloat16)
            own[2 * update + 1, rows, :] = (sigma_right * value_right).astype(jnp.bfloat16)
            saved[update, VALUE_LEFT, rows, :] = value_left
            saved[update, SIGMA_LEFT, rows, :] = sigma_left
            saved[update, VALUE_RIGHT, rows, :] = value_right
            saved[update, SIGMA_RIGHT, rows, :] = sigma_right
            saved[update, GATE, rows, :] = jax.nn.sigmoid(projected[rows, 4 * width :])

        in_chunks(gate_step)

    def widen(which, slot):
        landed(strips, which, slot, strip_send, strip_recv)

        def step(rows):
            wide[which, slot, rows, :] = strips[which, slot, rows, :].astype(jnp.float32)

        in_chunks(step)

    def contract(totals, spread, spread_major, stream, stream_major):
        half = 8

        def run(index, totals):
            totals = list(totals)
            for inner in range(half):
                t = index * half + inner
                if stream_major:
                    block = stream[pl.ds(pl.multiple_of(t * side, side), side), :]
                else:
                    block = stream[pl.ds(t, side, stride=side), :]
                for a in range(side):
                    place = t * side + a if spread_major else a * side + t
                    totals[a] = totals[a] + spread[pl.ds(place, 1), :] * block
            return tuple(totals)

        return lax.fori_loop(0, side // half, run, totals)

    def zeros():
        return tuple(jnp.zeros((side, pair_ref.shape[-1]), jnp.float32) for _ in range(side))

    def product(left, right, start, left_major, right_major):
        for a in range(side):
            work[a * side : (a + 1) * side, :] = jnp.zeros((side, work.shape[1]), jnp.float32)
        def step(index, carry):
            slot = turned(start, index)
            widen(left, slot)
            widen(right, slot)
            totals = tuple(work[a * side : (a + 1) * side, :] for a in range(side))
            totals = contract(
                totals, wide.at[left, slot], left_major, wide.at[right, slot], right_major
            )
            for a in range(side):
                work[a * side : (a + 1) * side, :] = totals[a]
            return carry

        lax.fori_loop(0, parts, step, 0)

    def output(update, cast):
        gain = gains_ref[update, 1:2, :]
        shift = shifts_ref[update, 1:2, :]

        def norm_step(rows):
            standard, inverse, normed = layer_norm(work[rows, :], gain, shift)
            saved[update, CENTRED, rows, :] = standard
            inverses[update, 1, rows, :] = jnp.broadcast_to(inverse, standard.shape)
            cast[rows, :] = normed.astype(jnp.bfloat16)

        in_chunks(norm_step)
        saved[update, HIDDEN] = matmul(cast[...], out_weights_ref[update])

    def output_back(update, cast):
        gain = gains_ref[update, 1:2, :]
        width = gain.shape[1]

        def gate_step(rows):
            incoming = upstream[rows, :]
            gate = saved[update, GATE, rows, :]
            gated = incoming * gate
            cast[rows, :] = gated.astype(jnp.bfloat16)
            term = gated * saved[update, HIDDEN, rows, :] * (1.0 - gate)
            pieces[rows, 4 * width :] = term.astype(jnp.bfloat16)

        in_chunks(gate_step)
        work[...] = matmul_transposed(cast[...], out_weights_ref[update])

        def norm_step(rows):
            grad = norm_backward(
                work[rows, :],
                saved[update, CENTRED, rows, :],
                inverses[update, 1, rows, :],
                gain,
            )
            work[rows, :] = grad.astype(jnp.bfloat16).astype(jnp.float32)

        in_chunks(norm_step)

    def partial(which, kind, operands):
        def make(step):
            _, tile, _ = route(kind, step)
            totals = contract(zeros(), *operands(tile))
            for a in range(side):
                partials[which, tile, a * side : (a + 1) * side, :] = totals[a].astype(jnp.bfloat16)
            ship(kind, step, partials.at[which, tile], sums, which, sum_send, sum_recv)

        return make

    def add_up(which):
        for slot in range(parts):
            landed(sums, which, slot, sum_send, sum_recv)

        def step(rows):
            total = sums[which, 0, rows, :].astype(jnp.float32)
            for slot in range(1, parts):
                total = total + sums[which, slot, rows, :].astype(jnp.float32)
            grads[which % 2, rows, :] = total
            edge_grads_ref[which, rows, :] = total.astype(jnp.bfloat16)

        in_chunks(step)

    def edges_back(update, finish):
        gain = gains_ref[update, 0:1, :]
        width = gain.shape[1]

        def piece_step(rows):
            for place, value, sigma in ((0, VALUE_LEFT, SIGMA_LEFT), (1, VALUE_RIGHT, SIGMA_RIGHT)):
                gate = saved[update, sigma, rows, :]
                scaled = grads[place, rows, :] * gate
                start = 2 * place * width
                pieces[rows, start : start + width] = scaled.astype(jnp.bfloat16)
                slope = scaled * saved[update, value, rows, :] * (1.0 - gate)
                pieces[rows, start + width : start + 2 * width] = slope.astype(jnp.bfloat16)

        in_chunks(piece_step)
        work[...] = matmul_transposed(pieces[...], edge_weights_ref[update])

        def norm_step(rows):
            finish(
                rows,
                norm_backward(
                    work[rows, :],
                    saved[update, STANDARD, rows, :],
                    inverses[update, 0, rows, :],
                    gain,
                ),
            )

        in_chunks(norm_step)

    def spread_strip(which, kind):
        for step in range(parts):
            ship(kind, step, own.at[which], strips, which, strip_send, strip_recv)

    cast = middle.at[1]
    project(0, pair_ref, cast)
    pl.semaphore_wait(barrier, others)
    spread_strip(LEFT_OUT, "row")
    spread_strip(RIGHT_OUT, "to_col")
    product(LEFT_OUT, RIGHT_OUT, col, False, False)
    output(0, cast)

    def middle_step(rows):
        update = saved[0, GATE, rows, :] * saved[0, HIDDEN, rows, :]
        middle[0, rows, :] = (pair_ref[rows, :].astype(jnp.float32) + update).astype(jnp.bfloat16)
        upstream[rows, :] = cotangent_ref[rows, :].astype(jnp.float32)

    in_chunks(middle_step)

    project(1, middle.at[0], cast)
    spread_strip(LEFT_IN, "to_row")
    spread_strip(RIGHT_IN, "col")
    product(LEFT_IN, RIGHT_IN, row, True, True)
    output(1, cast)
    output_back(1, cast)

    make_left = partial(
        LEFT_IN, "to_col", lambda tile: (wide.at[RIGHT_IN, tile], False, work, False)
    )
    make_right = partial(
        RIGHT_IN, "col", lambda tile: (wide.at[LEFT_IN, tile], False, work, True)
    )
    for step in list(range(1, parts)) + [0]:
        make_left(step)
        make_right(step)
    add_up(LEFT_IN)
    add_up(RIGHT_IN)

    def upstream_step(rows, grad):
        upstream[rows, :] = upstream[rows, :] + grad

    edges_back(1, upstream_step)
    output_back(0, cast)

    make_left = partial(
        LEFT_OUT, "row", lambda tile: (work, False, wide.at[RIGHT_OUT, tile], True)
    )
    make_right = partial(
        RIGHT_OUT, "to_row", lambda tile: (work, True, wide.at[LEFT_OUT, tile], True)
    )
    for step in list(range(1, parts)) + [0]:
        make_left(step)
        make_right(step)
    add_up(LEFT_OUT)
    add_up(RIGHT_OUT)

    def final_step(rows, grad):
        pair_grad_ref[rows, :] = (upstream[rows, :] + grad).astype(jnp.bfloat16)

    edges_back(0, final_step)

    strip_kinds = ("row", "to_col", "to_row", "col")
    sum_kinds = ("row", "to_row", "to_col", "col")
    for which in range(4):
        for step in range(parts):
            shipped(
                strip_kinds[which], step, own.at[which], strips, which, strip_send, strip_recv
            )
            _, tile, _ = route(sum_kinds[which], step)
            shipped(
                sum_kinds[which],
                step,
                partials.at[which, tile],
                sums,
                which,
                sum_send,
                sum_recv,
            )


def fused_body(pair, pair_cotangent, edge_weights, out_weights, norm_gains, norm_shifts):
    parts = lax.axis_size("row")
    side, _, width = pair.shape
    area = side * side
    tile = (area, width)
    vmem = pl.BlockSpec(memory_space=pltpu.VMEM)
    pair_grad, edge_grads = pl.pallas_call(
        functools.partial(kernel, parts, side),
        out_shape=(
            jax.ShapeDtypeStruct(tile, jnp.bfloat16),
            jax.ShapeDtypeStruct((4, *tile), jnp.bfloat16),
        ),
        in_specs=[vmem] * 6,
        out_specs=(vmem, vmem),
        scratch_shapes=[
            pltpu.VMEM((4, *tile), jnp.bfloat16),
            pltpu.VMEM((4, parts, *tile), jnp.bfloat16),
            pltpu.VMEM((4, parts, *tile), jnp.bfloat16),
            pltpu.VMEM((4, parts, *tile), jnp.bfloat16),
            pltpu.VMEM((4, parts, *tile), jnp.float32),
            pltpu.VMEM((2, 8, *tile), jnp.float32),
            pltpu.VMEM((2, 2, *tile), jnp.float32),
            pltpu.VMEM((area, edge_weights.shape[2]), jnp.float32),
            pltpu.VMEM(tile, jnp.float32),
            pltpu.VMEM((2, *tile), jnp.float32),
            pltpu.VMEM((2, *tile), jnp.bfloat16),
            pltpu.VMEM(tile, jnp.float32),
            pltpu.VMEM((area, edge_weights.shape[2]), jnp.bfloat16),
            pltpu.SemaphoreType.DMA((4, parts)),
            pltpu.SemaphoreType.DMA((4, parts)),
            pltpu.SemaphoreType.DMA((4, parts)),
            pltpu.SemaphoreType.DMA((4, parts)),
        ],
        compiler_params=pltpu.CompilerParams(
            collective_id=0, has_side_effects=True, vmem_limit_bytes=40 * 1024 * 1024
        ),
    )(
        pair.reshape(tile),
        pair_cotangent.reshape(tile),
        edge_weights,
        out_weights,
        norm_gains,
        norm_shifts,
    )
    return pair_grad.reshape(pair.shape), edge_grads.reshape(4, *pair.shape)


def body(pair, pair_cotangent, edge_weights, out_weights, norm_gains, norm_shifts):
    arguments = (pair, pair_cotangent, edge_weights, out_weights, norm_gains, norm_shifts)
    square = lax.axis_size("row") == lax.axis_size("col") and pair.shape[0] == pair.shape[1]
    if square and pair.shape[0] % 16 == 0:
        return fused_body(*arguments)
    return gathered_body(*arguments)


def solution(mesh):
    return jax.shard_map(
        body,
        mesh=mesh,
        in_specs=(
            P(("groups", "row"), "col", None),
            P(("groups", "row"), "col", None),
            P(),
            P(),
            P(),
            P(),
        ),
        out_specs=(P(("groups", "row"), "col", None), P(None, ("groups", "row"), "col", None)),
        check_vma=False,
    )
```

```python
import functools

import jax
import jax.numpy as jnp
from jax import lax
from jax.experimental import pallas as pl
from jax.experimental.pallas import tpu as pltpu
from jax.sharding import PartitionSpec as P

EPSILON = 1e-05


def product_of(form, left, right):
    return jnp.einsum(form, left, right, preferred_element_type=jnp.float32)


def layer_norm(inputs, norm_gain, norm_shift):
    centre = jnp.mean(inputs, axis=-1, keepdims=True)
    centred = inputs - centre
    inverse = lax.rsqrt(jnp.mean(centred * centred, axis=-1, keepdims=True) + EPSILON)
    standard = centred * inverse
    return (standard, inverse, standard * norm_gain + norm_shift)


def norm_backward(upstream, standard, inverse, norm_gain):
    scaled = upstream * norm_gain
    mean_grad = jnp.mean(scaled, axis=-1, keepdims=True)
    second = jnp.mean(scaled * standard, axis=-1, keepdims=True)
    return (scaled - mean_grad - standard * second) * inverse


def edges_forward(inputs, weights, norm_gain, norm_shift):
    standard, inverse, normed = layer_norm(inputs, norm_gain, norm_shift)
    projected = product_of("ijc,cd->ijd", normed.astype(jnp.bfloat16), weights)
    width = weights.shape[1] // 5
    value_left = projected[..., :width]
    sigma_left = jax.nn.sigmoid(projected[..., width : 2 * width])
    value_right = projected[..., 2 * width : 3 * width]
    sigma_right = jax.nn.sigmoid(projected[..., 3 * width : 4 * width])
    out_gate = jax.nn.sigmoid(projected[..., 4 * width :])
    left_edge = (sigma_left * value_left).astype(jnp.bfloat16)
    right_edge = (sigma_right * value_right).astype(jnp.bfloat16)
    saved = (standard, inverse, value_left, sigma_left, value_right, sigma_right, out_gate)
    return (left_edge, right_edge, saved)


def output_forward(product, out_weight, norm_gain, norm_shift):
    standard, inverse, normed = layer_norm(product, norm_gain, norm_shift)
    hidden_out = product_of("ijd,dc->ijc", normed.astype(jnp.bfloat16), out_weight)
    return (hidden_out, standard, inverse)


def output_backward(upstream, out_weight, norm_gain, out_gate, stats):
    hidden_out, standard, inverse = stats
    grad_hidden = (upstream * out_gate).astype(jnp.bfloat16)
    gate_term = upstream * hidden_out * out_gate * (1.0 - out_gate)
    grad_normed = product_of("ijc,dc->ijd", grad_hidden, out_weight)
    grad_product = norm_backward(grad_normed, standard, inverse, norm_gain).astype(jnp.bfloat16)
    return (grad_product, gate_term)


def edges_backward(grad_left, grad_right, gate_term, weights, norm_gain, saved):
    standard, inverse, value_left, sigma_left, value_right, sigma_right, out_gate = saved
    pieces = jnp.concatenate(
        [
            grad_left * sigma_left,
            grad_left * value_left * sigma_left * (1.0 - sigma_left),
            grad_right * sigma_right,
            grad_right * value_right * sigma_right * (1.0 - sigma_right),
            gate_term,
        ],
        axis=-1,
    )
    grad_normed = product_of("ijd,cd->ijc", pieces.astype(jnp.bfloat16), weights)
    return norm_backward(grad_normed, standard, inverse, norm_gain)


def row_strip(tile):
    return lax.all_gather(tile, "col", axis=1, tiled=True)


def column_strip(tile):
    return lax.all_gather(tile, "row", axis=0, tiled=True)


def shuffle_rows(tile):
    return lax.all_to_all(tile, "row", split_axis=1, concat_axis=0, tiled=True)


def shuffle_columns(tile):
    return lax.all_to_all(tile, "col", split_axis=0, concat_axis=1, tiled=True)


def transposed_columns(tile):
    row_devices = lax.axis_size("row")
    column_devices = lax.axis_size("col")
    moved = shuffle_columns(shuffle_rows(tile))
    gathered = column_strip(jnp.swapaxes(moved, 0, 1))
    total = gathered.shape[0]
    block = total // (row_devices * column_devices)
    gathered = gathered.reshape(
        row_devices, column_devices, block, gathered.shape[1], gathered.shape[2]
    )
    return jnp.swapaxes(gathered, 0, 1).reshape(total, gathered.shape[3], gathered.shape[4])


def transposed_rows(tile):
    row_devices = lax.axis_size("row")
    column_devices = lax.axis_size("col")
    moved = shuffle_rows(shuffle_columns(tile))
    gathered = row_strip(jnp.swapaxes(moved, 0, 1))
    total = gathered.shape[1]
    block = total // (row_devices * column_devices)
    gathered = gathered.reshape(
        gathered.shape[0], column_devices, row_devices, block, gathered.shape[2]
    )
    return jnp.swapaxes(gathered, 1, 2).reshape(gathered.shape[0], total, gathered.shape[4])


def gathered_body(pair, pair_cotangent, edge_weights, out_weights, norm_gains, norm_shifts):
    pair_float = pair.astype(jnp.float32)
    left_out, right_out, saved_out = edges_forward(
        pair_float, edge_weights[0], norm_gains[0, 0], norm_shifts[0, 0]
    )
    strip_right = column_strip(right_out)
    product_out = product_of("ikc,kjc->ijc", row_strip(left_out), transposed_columns(right_out))
    stats_out = output_forward(product_out, out_weights[0], norm_gains[0, 1], norm_shifts[0, 1])
    middle = (pair_float + saved_out[6] * stats_out[0]).astype(jnp.bfloat16)
    left_in, right_in, saved_in = edges_forward(
        middle.astype(jnp.float32), edge_weights[1], norm_gains[1, 0], norm_shifts[1, 0]
    )
    product_in = product_of("ikc,kjc->ijc", transposed_rows(left_in), column_strip(right_in))
    stats_in = output_forward(product_in, out_weights[1], norm_gains[1, 1], norm_shifts[1, 1])
    upstream = pair_cotangent.astype(jnp.float32)
    grad_product_in, gate_in = output_backward(
        upstream, out_weights[1], norm_gains[1, 1], saved_in[6], stats_in
    )
    grad_left_in = product_of(
        "kjc,jic->kic", row_strip(right_in), transposed_columns(grad_product_in)
    )
    grad_right_in = product_of("kic,ijc->kjc", row_strip(left_in), column_strip(grad_product_in))
    grad_middle = upstream + edges_backward(
        grad_left_in, grad_right_in, gate_in, edge_weights[1], norm_gains[1, 0], saved_in
    )
    grad_product_out, gate_outer = output_backward(
        grad_middle, out_weights[0], norm_gains[0, 1], saved_out[6], stats_out
    )
    grad_left_out = product_of("ijc,jkc->ikc", row_strip(grad_product_out), strip_right)
    grad_right_out = product_of(
        "jic,ikc->jkc", transposed_rows(grad_product_out), column_strip(left_out)
    )
    pair_grad = grad_middle + edges_backward(
        grad_left_out, grad_right_out, gate_outer, edge_weights[0], norm_gains[0, 0], saved_out
    )
    edge_grads = jnp.stack([grad_left_out, grad_right_out, grad_left_in, grad_right_in])
    return (pair_grad.astype(jnp.bfloat16), edge_grads.astype(jnp.bfloat16))


MESH = pl.DeviceIdType.MESH
RIGHT_OUT, LEFT_IN, GRAD_IN, GRAD_OUT = range(4)
PRODUCT_OUT, PRODUCT_IN, SUM_LEFT_IN, SUM_RIGHT_OUT = range(4)
STRIP_AXIS = ("col", "row", "col", "row")
SUM_AXIS = ("row", "col", "row", "col")
STANDARD, VALUE_LEFT, SIGMA_LEFT, VALUE_RIGHT, SIGMA_RIGHT, GATE, CENTRED = range(7)


def matmul(left, right):
    return jnp.dot(left, right, preferred_element_type=jnp.float32)


def matmul_transposed(left, right):
    return lax.dot_general(
        left, right, (((1,), (1,)), ((), ())), preferred_element_type=jnp.float32
    )


def kernel(
    parts,
    side,
    pair_hbm,
    cotangent_hbm,
    edge_weights_hbm,
    out_weights_hbm,
    gains_hbm,
    shifts_hbm,
    pair_grad_ref,
    edge_grads_ref,
    pair_ref,
    cotangent_ref,
    edge_weights_ref,
    out_weights_ref,
    gains_ref,
    shifts_ref,
    own,
    strips,
    partials,
    sums,
    wide,
    single,
    saved,
    inverses,
    projected,
    work,
    extra,
    grads,
    middle,
    cast,
    upstream,
    pieces,
    load_sem,
    strip_send,
    strip_recv,
    sum_send,
    sum_recv,
):
    row = lax.axis_index("row")
    col = lax.axis_index("col")
    area = side * side
    width = pair_ref.shape[1]
    chunk = min(area, 64)
    place_of = {"row": col, "col": row}

    def turned(index, step):
        return lax.rem(index + parts + step, parts)

    def device_along(axis, place):
        return {"row": row, "col": place} if axis == "row" else {"row": place, "col": col}

    barrier = pltpu.get_barrier_semaphore()
    for axis in ("row", "col"):
        for step in range(1, parts):
            pl.semaphore_signal(
                barrier,
                inc=1,
                device_id=device_along(axis, turned(place_of[axis], step)),
                device_id_type=MESH,
            )

    loads = [
        pltpu.make_async_copy(source, target, load_sem.at[index])
        for index, (source, target) in enumerate(
            (
                (pair_hbm, pair_ref),
                (gains_hbm, gains_ref),
                (shifts_hbm, shifts_ref),
                (edge_weights_hbm, edge_weights_ref),
                (out_weights_hbm, out_weights_ref),
                (cotangent_hbm, cotangent_ref),
            )
        )
    ]
    for load in loads:
        load.start()

    def in_chunks(step):
        def run(index, carry):
            step(pl.ds(pl.multiple_of(index * chunk, chunk), chunk))
            return carry

        lax.fori_loop(0, area // chunk, run, 0)

    def strip_copy(which, step):
        axis = STRIP_AXIS[which]
        return pltpu.make_async_remote_copy(
            src_ref=own.at[which],
            dst_ref=strips.at[which, place_of[axis]],
            send_sem=strip_send.at[which, step],
            recv_sem=strip_recv.at[which, place_of[axis]],
            device_id=device_along(axis, turned(place_of[axis], step)),
            device_id_type=MESH,
        )

    def send_strip(which):
        for step in range(1, parts):
            strip_copy(which, step).start()

    def take_strip(which, slot):
        pltpu.make_async_remote_copy(
            src_ref=own.at[which],
            dst_ref=strips.at[which, slot],
            send_sem=strip_send.at[which, 0],
            recv_sem=strip_recv.at[which, slot],
            device_id=device_along("row", col),
            device_id_type=MESH,
        ).wait_recv()

        def step(rows):
            wide[which, slot, rows, :] = strips[which, slot, rows, :].astype(jnp.float32)

        in_chunks(step)

    def sum_copy(which, tile):
        axis = SUM_AXIS[which]
        return pltpu.make_async_remote_copy(
            src_ref=partials.at[which, tile],
            dst_ref=sums.at[which, place_of[axis]],
            send_sem=sum_send.at[which, tile],
            recv_sem=sum_recv.at[which, place_of[axis]],
            device_id=device_along(axis, tile),
            device_id_type=MESH,
        )

    def send_sum(which, tile, totals):
        for a in range(side):
            partials[which, tile, a * side : (a + 1) * side, :] = totals[a].astype(jnp.bfloat16)

        @pl.when(tile != place_of[SUM_AXIS[which]])
        def _():
            sum_copy(which, tile).start()

    def added(which):
        place = place_of[SUM_AXIS[which]]
        for step in range(1, parts):
            slot = turned(place, -step)
            pltpu.make_async_remote_copy(
                src_ref=partials.at[which, 0],
                dst_ref=sums.at[which, slot],
                send_sem=sum_send.at[which, 0],
                recv_sem=sum_recv.at[which, slot],
                device_id=device_along("row", col),
                device_id_type=MESH,
            ).wait_recv()

        def read(rows):
            total = partials[which, place, rows, :].astype(jnp.float32)
            for step in range(1, parts):
                slot = turned(place, step)
                total = total + sums[which, slot, rows, :].astype(jnp.float32)
            return total

        return read

    def contract(totals, spread, spread_major, stream, stream_major):
        half = 8

        def run(index, totals):
            totals = list(totals)
            for inner in range(half):
                t = index * half + inner
                if stream_major:
                    block = stream[pl.ds(pl.multiple_of(t * side, side), side), :]
                else:
                    block = stream[pl.ds(t, side, stride=side), :]
                for a in range(side):
                    place = t * side + a if spread_major else a * side + t
                    totals[a] = totals[a] + spread[pl.ds(place, 1), :] * block
            return tuple(totals)

        return lax.fori_loop(0, side // half, run, totals)

    def zeros():
        return tuple(jnp.zeros((side, width), jnp.float32) for _ in range(side))

    def over_strip(which, step):
        place = place_of[STRIP_AXIS[which]]
        step(place, True)

        def run(index, carry):
            slot = turned(place, -index)
            take_strip(which, slot)
            step(slot, False)
            return carry

        lax.fori_loop(1, parts, run, 0)

    def put(target, totals):
        for a in range(side):
            target[a * side : (a + 1) * side, :] = totals[a]

    def grow(target, first, operands):
        totals = tuple(target[a * side : (a + 1) * side, :] for a in range(side))
        if first:
            totals = zeros()
        put(target, contract(totals, *operands))

    def norm_in(update, source):
        gain = gains_ref[update, 0:1, :]
        shift = shifts_ref[update, 0:1, :]

        def step(rows):
            inputs = source[rows, :].astype(jnp.float32)
            standard, inverse, normed = layer_norm(inputs, gain, shift)
            saved[update, STANDARD, rows, :] = standard
            inverses[update, 0, rows, :] = jnp.broadcast_to(inverse, standard.shape)
            cast[rows, :] = normed.astype(jnp.bfloat16)

        in_chunks(step)

    def project(update, start, stop):
        projected[:, start:stop] = matmul(cast[...], edge_weights_ref[update, :, start:stop])

    def edge(update, side_of, rows):
        start = 2 * side_of * width
        value = projected[rows, start : start + width]
        sigma = jax.nn.sigmoid(projected[rows, start + width : start + 2 * width])
        saved[update, VALUE_LEFT + 2 * side_of, rows, :] = value
        saved[update, SIGMA_LEFT + 2 * side_of, rows, :] = sigma
        return (sigma * value).astype(jnp.bfloat16)

    def gate_out(update, rows):
        gate = jax.nn.sigmoid(projected[rows, 4 * width :])
        saved[update, GATE, rows, :] = gate

    def pass_back(update):
        def step(rows):
            gated = upstream[rows, :] * saved[update, GATE, rows, :]
            cast[rows, :] = gated.astype(jnp.bfloat16)

        in_chunks(step)
        work[...] = matmul_transposed(cast[...], out_weights_ref[update])

    def product_back(update, which, rows, standard, inverse):
        grad = norm_backward(work[rows, :], standard, inverse, gains_ref[update, 1:2, :])
        grad = grad.astype(jnp.bfloat16)
        own[which, rows, :] = grad
        place = place_of[STRIP_AXIS[which]]
        wide[which, place, rows, :] = grad.astype(jnp.float32)

    def gate_piece(update, hidden):
        def step(rows):
            gate = saved[update, GATE, rows, :]
            term = upstream[rows, :] * hidden[rows, :] * gate * (1.0 - gate)
            pieces[rows, 4 * width :] = term.astype(jnp.bfloat16)

        in_chunks(step)

    def edge_pieces(update, side_of, rows, grad):
        value = saved[update, VALUE_LEFT + 2 * side_of, rows, :]
        sigma = saved[update, SIGMA_LEFT + 2 * side_of, rows, :]
        scaled = grad * sigma
        slope = scaled * value * (1.0 - sigma)
        start = 2 * side_of * width
        pieces[rows, start : start + width] = scaled.astype(jnp.bfloat16)
        pieces[rows, start + width : start + 2 * width] = slope.astype(jnp.bfloat16)
        edge_grads_ref[2 * update + side_of, rows, :] = grad.astype(jnp.bfloat16)

    def pieces_back(update, start, stop):
        return matmul_transposed(pieces[:, start:stop], edge_weights_ref[update, :, start:stop])

    def input_back(update, rows):
        return norm_backward(
            work[rows, :],
            saved[update, STANDARD, rows, :],
            inverses[update, 0, rows, :],
            gains_ref[update, 0:1, :],
        )

    for load in loads[:3]:
        load.wait()
    norm_in(0, pair_ref)
    loads[3].wait()
    project(0, 2 * width, 4 * width)

    def right_out_step(rows):
        right = edge(0, 1, rows)
        own[RIGHT_OUT, rows, :] = right
        wide[RIGHT_OUT, row, rows, :] = right.astype(jnp.float32)

    in_chunks(right_out_step)
    pl.semaphore_wait(barrier, 2 * (parts - 1))
    send_strip(RIGHT_OUT)
    project(0, 0, 2 * width)

    def left_out_step(rows):
        single[0, rows, :] = edge(0, 0, rows).astype(jnp.float32)

    in_chunks(left_out_step)

    def product_out_step(slot, first):
        totals = contract(zeros(), single.at[0], False, wide.at[RIGHT_OUT, slot], False)
        send_sum(PRODUCT_OUT, slot, totals)

    over_strip(RIGHT_OUT, product_out_step)
    project(0, 4 * width, 5 * width)
    loads[4].wait()
    loads[5].wait()

    def gate_step(rows):
        gate_out(0, rows)
        upstream[rows, :] = cotangent_ref[rows, :].astype(jnp.float32)

    in_chunks(gate_step)

    total_out = added(PRODUCT_OUT)

    def norm_out_step(rows):
        standard, inverse, normed = layer_norm(
            total_out(rows), gains_ref[0, 1:2, :], shifts_ref[0, 1:2, :]
        )
        saved[0, CENTRED, rows, :] = standard
        inverses[0, 1, rows, :] = jnp.broadcast_to(inverse, standard.shape)
        cast[rows, :] = normed.astype(jnp.bfloat16)

    in_chunks(norm_out_step)
    extra[0] = matmul(cast[...], out_weights_ref[0])

    def middle_step(rows):
        update = saved[0, GATE, rows, :] * extra[0, rows, :]
        middle[rows, :] = (pair_ref[rows, :].astype(jnp.float32) + update).astype(jnp.bfloat16)

    in_chunks(middle_step)

    norm_in(1, middle)
    project(1, 0, 2 * width)

    def left_in_step(rows):
        left = edge(1, 0, rows)
        own[LEFT_IN, rows, :] = left
        wide[LEFT_IN, col, rows, :] = left.astype(jnp.float32)

    in_chunks(left_in_step)
    send_strip(LEFT_IN)
    project(1, 2 * width, 5 * width)

    def right_in_step(rows):
        single[1, rows, :] = edge(1, 1, rows).astype(jnp.float32)

    in_chunks(right_in_step)

    def product_in_step(slot, first):
        totals = contract(zeros(), wide.at[LEFT_IN, slot], True, single.at[1], True)
        send_sum(PRODUCT_IN, slot, totals)

    over_strip(LEFT_IN, product_in_step)
    in_chunks(functools.partial(gate_out, 1))
    pass_back(1)

    total_in = added(PRODUCT_IN)

    def norm_in_step(rows):
        standard, inverse, normed = layer_norm(
            total_in(rows), gains_ref[1, 1:2, :], shifts_ref[1, 1:2, :]
        )
        cast[rows, :] = normed.astype(jnp.bfloat16)
        product_back(1, GRAD_IN, rows, standard, inverse)

    in_chunks(norm_in_step)
    send_strip(GRAD_IN)
    extra[1] = matmul(cast[...], out_weights_ref[1])
    gate_piece(1, extra.at[1])

    def left_in_back(slot, first):
        totals = contract(zeros(), single.at[1], False, wide.at[GRAD_IN, slot], False)
        send_sum(SUM_LEFT_IN, slot, totals)

    over_strip(GRAD_IN, left_in_back)
    for slot in range(parts):
        grow(
            grads,
            slot == 0,
            (wide.at[LEFT_IN, slot], False, wide.at[GRAD_IN, slot], True),
        )
    in_chunks(lambda rows: edge_pieces(1, 1, rows, grads[rows, :]))
    work[...] = pieces_back(1, 2 * width, 5 * width)
    sum_left_in = added(SUM_LEFT_IN)
    in_chunks(lambda rows: edge_pieces(1, 0, rows, sum_left_in(rows)))
    work[...] = work[...] + pieces_back(1, 0, 2 * width)

    def grad_middle_step(rows):
        upstream[rows, :] = upstream[rows, :] + input_back(1, rows)

    in_chunks(grad_middle_step)

    pass_back(0)

    def product_out_back(rows):
        product_back(0, GRAD_OUT, rows, saved[0, CENTRED, rows, :], inverses[0, 1, rows, :])

    in_chunks(product_out_back)
    send_strip(GRAD_OUT)
    gate_piece(0, extra.at[0])

    def right_out_back(slot, first):
        totals = contract(zeros(), wide.at[GRAD_OUT, slot], True, single.at[0], True)
        send_sum(SUM_RIGHT_OUT, slot, totals)

    over_strip(GRAD_OUT, right_out_back)
    for slot in range(parts):
        grow(
            grads,
            slot == 0,
            (wide.at[GRAD_OUT, slot], False, wide.at[RIGHT_OUT, slot], True),
        )
    in_chunks(lambda rows: edge_pieces(0, 0, rows, grads[rows, :]))
    work[...] = pieces_back(0, 0, 2 * width) + pieces_back(0, 4 * width, 5 * width)
    sum_right_out = added(SUM_RIGHT_OUT)
    in_chunks(lambda rows: edge_pieces(0, 1, rows, sum_right_out(rows)))
    work[...] = work[...] + pieces_back(0, 2 * width, 4 * width)

    def final_step(rows):
        total = upstream[rows, :] + input_back(0, rows)
        pair_grad_ref[rows, :] = total.astype(jnp.bfloat16)

    in_chunks(final_step)

    for which in range(4):
        for step in range(1, parts):
            strip_copy(which, step).wait_send()
            tile = turned(place_of[SUM_AXIS[which]], step)
            sum_copy(which, tile).wait_send()


def fused_body(pair, pair_cotangent, edge_weights, out_weights, norm_gains, norm_shifts):
    parts = lax.axis_size("row")
    side, _, width = pair.shape
    area = side * side
    tile = (area, width)
    arguments = (
        pair.reshape(tile),
        pair_cotangent.reshape(tile),
        edge_weights,
        out_weights,
        norm_gains,
        norm_shifts,
    )
    vmem = pl.BlockSpec(memory_space=pltpu.VMEM)
    semaphores = pltpu.SemaphoreType.DMA((4, parts))
    pair_grad, edge_grads = pl.pallas_call(
        functools.partial(kernel, parts, side),
        out_shape=(
            jax.ShapeDtypeStruct(tile, jnp.bfloat16),
            jax.ShapeDtypeStruct((4, *tile), jnp.bfloat16),
        ),
        in_specs=[pl.BlockSpec(memory_space=pltpu.HBM)] * 6,
        out_specs=(vmem, vmem),
        scratch_shapes=[
            *(pltpu.VMEM(argument.shape, argument.dtype) for argument in arguments),
            pltpu.VMEM((4, *tile), jnp.bfloat16),
            pltpu.VMEM((4, parts, *tile), jnp.bfloat16),
            pltpu.VMEM((4, parts, *tile), jnp.bfloat16),
            pltpu.VMEM((4, parts, *tile), jnp.bfloat16),
            pltpu.VMEM((4, parts, *tile), jnp.float32),
            pltpu.VMEM((2, *tile), jnp.float32),
            pltpu.VMEM((2, 7, *tile), jnp.float32),
            pltpu.VMEM((2, 2, *tile), jnp.float32),
            pltpu.VMEM((area, edge_weights.shape[2]), jnp.float32),
            pltpu.VMEM(tile, jnp.float32),
            pltpu.VMEM((2, *tile), jnp.float32),
            pltpu.VMEM(tile, jnp.float32),
            pltpu.VMEM(tile, jnp.bfloat16),
            pltpu.VMEM(tile, jnp.bfloat16),
            pltpu.VMEM(tile, jnp.float32),
            pltpu.VMEM((area, edge_weights.shape[2]), jnp.bfloat16),
            pltpu.SemaphoreType.DMA((len(arguments),)),
            semaphores,
            semaphores,
            semaphores,
            semaphores,
        ],
        compiler_params=pltpu.CompilerParams(
            collective_id=0, has_side_effects=True, vmem_limit_bytes=40 * 1024 * 1024
        ),
    )(*arguments)
    return pair_grad.reshape(pair.shape), edge_grads.reshape(4, *pair.shape)


def body(pair, pair_cotangent, edge_weights, out_weights, norm_gains, norm_shifts):
    arguments = (pair, pair_cotangent, edge_weights, out_weights, norm_gains, norm_shifts)
    square = lax.axis_size("row") == lax.axis_size("col") and pair.shape[0] == pair.shape[1]
    if square and pair.shape[0] % 16 == 0:
        return fused_body(*arguments)
    return gathered_body(*arguments)


def solution(mesh):
    return jax.shard_map(
        body,
        mesh=mesh,
        in_specs=(
            P(("groups", "row"), "col", None),
            P(("groups", "row"), "col", None),
            P(),
            P(),
            P(),
            P(),
        ),
        out_specs=(P(("groups", "row"), "col", None), P(None, ("groups", "row"), "col", None)),
        check_vma=False,
    )
```

```python
import functools

import jax
import jax.numpy as jnp
from jax import lax
from jax.experimental import pallas as pl
from jax.experimental.pallas import tpu as pltpu
from jax.sharding import PartitionSpec as P

EPSILON = 1e-05


def product_of(form, left, right):
    return jnp.einsum(form, left, right, preferred_element_type=jnp.float32)


def layer_norm(inputs, norm_gain, norm_shift):
    centre = jnp.mean(inputs, axis=-1, keepdims=True)
    centred = inputs - centre
    inverse = lax.rsqrt(jnp.mean(centred * centred, axis=-1, keepdims=True) + EPSILON)
    standard = centred * inverse
    return (standard, inverse, standard * norm_gain + norm_shift)


def norm_backward(upstream, standard, inverse, norm_gain):
    scaled = upstream * norm_gain
    mean_grad = jnp.mean(scaled, axis=-1, keepdims=True)
    second = jnp.mean(scaled * standard, axis=-1, keepdims=True)
    return (scaled - mean_grad - standard * second) * inverse


def edges_forward(inputs, weights, norm_gain, norm_shift):
    standard, inverse, normed = layer_norm(inputs, norm_gain, norm_shift)
    projected = product_of("ijc,cd->ijd", normed.astype(jnp.bfloat16), weights)
    width = weights.shape[1] // 5
    value_left = projected[..., :width]
    sigma_left = jax.nn.sigmoid(projected[..., width : 2 * width])
    value_right = projected[..., 2 * width : 3 * width]
    sigma_right = jax.nn.sigmoid(projected[..., 3 * width : 4 * width])
    out_gate = jax.nn.sigmoid(projected[..., 4 * width :])
    left_edge = (sigma_left * value_left).astype(jnp.bfloat16)
    right_edge = (sigma_right * value_right).astype(jnp.bfloat16)
    saved = (standard, inverse, value_left, sigma_left, value_right, sigma_right, out_gate)
    return (left_edge, right_edge, saved)


def output_forward(product, out_weight, norm_gain, norm_shift):
    standard, inverse, normed = layer_norm(product, norm_gain, norm_shift)
    hidden_out = product_of("ijd,dc->ijc", normed.astype(jnp.bfloat16), out_weight)
    return (hidden_out, standard, inverse)


def output_backward(upstream, out_weight, norm_gain, out_gate, stats):
    hidden_out, standard, inverse = stats
    grad_hidden = (upstream * out_gate).astype(jnp.bfloat16)
    gate_term = upstream * hidden_out * out_gate * (1.0 - out_gate)
    grad_normed = product_of("ijc,dc->ijd", grad_hidden, out_weight)
    grad_product = norm_backward(grad_normed, standard, inverse, norm_gain).astype(jnp.bfloat16)
    return (grad_product, gate_term)


def edges_backward(grad_left, grad_right, gate_term, weights, norm_gain, saved):
    standard, inverse, value_left, sigma_left, value_right, sigma_right, out_gate = saved
    pieces = jnp.concatenate(
        [
            grad_left * sigma_left,
            grad_left * value_left * sigma_left * (1.0 - sigma_left),
            grad_right * sigma_right,
            grad_right * value_right * sigma_right * (1.0 - sigma_right),
            gate_term,
        ],
        axis=-1,
    )
    grad_normed = product_of("ijd,cd->ijc", pieces.astype(jnp.bfloat16), weights)
    return norm_backward(grad_normed, standard, inverse, norm_gain)


def row_strip(tile):
    return lax.all_gather(tile, "col", axis=1, tiled=True)


def column_strip(tile):
    return lax.all_gather(tile, "row", axis=0, tiled=True)


def shuffle_rows(tile):
    return lax.all_to_all(tile, "row", split_axis=1, concat_axis=0, tiled=True)


def shuffle_columns(tile):
    return lax.all_to_all(tile, "col", split_axis=0, concat_axis=1, tiled=True)


def transposed_columns(tile):
    row_devices = lax.axis_size("row")
    column_devices = lax.axis_size("col")
    moved = shuffle_columns(shuffle_rows(tile))
    gathered = column_strip(jnp.swapaxes(moved, 0, 1))
    total = gathered.shape[0]
    block = total // (row_devices * column_devices)
    gathered = gathered.reshape(
        row_devices, column_devices, block, gathered.shape[1], gathered.shape[2]
    )
    return jnp.swapaxes(gathered, 0, 1).reshape(total, gathered.shape[3], gathered.shape[4])


def transposed_rows(tile):
    row_devices = lax.axis_size("row")
    column_devices = lax.axis_size("col")
    moved = shuffle_rows(shuffle_columns(tile))
    gathered = row_strip(jnp.swapaxes(moved, 0, 1))
    total = gathered.shape[1]
    block = total // (row_devices * column_devices)
    gathered = gathered.reshape(
        gathered.shape[0], column_devices, row_devices, block, gathered.shape[2]
    )
    return jnp.swapaxes(gathered, 1, 2).reshape(gathered.shape[0], total, gathered.shape[4])


def gathered_body(pair, pair_cotangent, edge_weights, out_weights, norm_gains, norm_shifts):
    pair_float = pair.astype(jnp.float32)
    left_out, right_out, saved_out = edges_forward(
        pair_float, edge_weights[0], norm_gains[0, 0], norm_shifts[0, 0]
    )
    strip_right = column_strip(right_out)
    product_out = product_of("ikc,kjc->ijc", row_strip(left_out), transposed_columns(right_out))
    stats_out = output_forward(product_out, out_weights[0], norm_gains[0, 1], norm_shifts[0, 1])
    middle = (pair_float + saved_out[6] * stats_out[0]).astype(jnp.bfloat16)
    left_in, right_in, saved_in = edges_forward(
        middle.astype(jnp.float32), edge_weights[1], norm_gains[1, 0], norm_shifts[1, 0]
    )
    product_in = product_of("ikc,kjc->ijc", transposed_rows(left_in), column_strip(right_in))
    stats_in = output_forward(product_in, out_weights[1], norm_gains[1, 1], norm_shifts[1, 1])
    upstream = pair_cotangent.astype(jnp.float32)
    grad_product_in, gate_in = output_backward(
        upstream, out_weights[1], norm_gains[1, 1], saved_in[6], stats_in
    )
    grad_left_in = product_of(
        "kjc,jic->kic", row_strip(right_in), transposed_columns(grad_product_in)
    )
    grad_right_in = product_of("kic,ijc->kjc", row_strip(left_in), column_strip(grad_product_in))
    grad_middle = upstream + edges_backward(
        grad_left_in, grad_right_in, gate_in, edge_weights[1], norm_gains[1, 0], saved_in
    )
    grad_product_out, gate_outer = output_backward(
        grad_middle, out_weights[0], norm_gains[0, 1], saved_out[6], stats_out
    )
    grad_left_out = product_of("ijc,jkc->ikc", row_strip(grad_product_out), strip_right)
    grad_right_out = product_of(
        "jic,ikc->jkc", transposed_rows(grad_product_out), column_strip(left_out)
    )
    pair_grad = grad_middle + edges_backward(
        grad_left_out, grad_right_out, gate_outer, edge_weights[0], norm_gains[0, 0], saved_out
    )
    edge_grads = jnp.stack([grad_left_out, grad_right_out, grad_left_in, grad_right_in])
    return (pair_grad.astype(jnp.bfloat16), edge_grads.astype(jnp.bfloat16))


MESH = pl.DeviceIdType.MESH
RIGHT_OUT, LEFT_IN, GRAD_IN, GRAD_OUT = range(4)
PRODUCT_OUT, PRODUCT_IN, SUM_LEFT_IN, SUM_RIGHT_OUT = range(4)
STRIP_AXIS = ("col", "row", "col", "row")
SUM_AXIS = ("row", "col", "row", "col")
STANDARD, VALUE_LEFT, SIGMA_LEFT, VALUE_RIGHT, SIGMA_RIGHT, GATE, CENTRED = range(7)


def matmul(left, right):
    return jnp.dot(left, right, preferred_element_type=jnp.float32)


def matmul_transposed(left, right):
    return lax.dot_general(
        left, right, (((1,), (1,)), ((), ())), preferred_element_type=jnp.float32
    )


def kernel(
    parts,
    side,
    pair_hbm,
    cotangent_hbm,
    edge_weights_hbm,
    out_weights_hbm,
    gains_hbm,
    shifts_hbm,
    pair_grad_ref,
    edge_grads_ref,
    pair_ref,
    cotangent_ref,
    edge_weights_ref,
    out_weights_ref,
    gains_ref,
    shifts_ref,
    own,
    strips,
    partials,
    sums,
    wide,
    single,
    saved,
    inverses,
    projected,
    work,
    extra,
    grads,
    middle,
    cast,
    upstream,
    pieces,
    load_sem,
    strip_send,
    strip_recv,
    sum_send,
    sum_recv,
):
    row = lax.axis_index("row")
    col = lax.axis_index("col")
    area = side * side
    width = pair_ref.shape[1]
    chunk = min(area, 128)
    place_of = {"row": col, "col": row}

    def turned(index, step):
        return lax.rem(index + parts + step, parts)

    def device_along(axis, place):
        return {"row": row, "col": place} if axis == "row" else {"row": place, "col": col}

    barrier = pltpu.get_barrier_semaphore()
    for axis in ("row", "col"):
        for step in range(1, parts):
            pl.semaphore_signal(
                barrier,
                inc=1,
                device_id=device_along(axis, turned(place_of[axis], step)),
                device_id_type=MESH,
            )

    loads = [
        pltpu.make_async_copy(source, target, load_sem.at[index])
        for index, (source, target) in enumerate(
            (
                (pair_hbm, pair_ref),
                (gains_hbm, gains_ref),
                (shifts_hbm, shifts_ref),
                (edge_weights_hbm, edge_weights_ref),
                (out_weights_hbm, out_weights_ref),
                (cotangent_hbm, cotangent_ref),
            )
        )
    ]
    for load in loads:
        load.start()

    def in_chunks(step):
        for start in range(0, area, chunk):
            step(pl.ds(start, chunk))

    def strip_copy(which, step):
        axis = STRIP_AXIS[which]
        return pltpu.make_async_remote_copy(
            src_ref=own.at[which],
            dst_ref=strips.at[which, place_of[axis]],
            send_sem=strip_send.at[which, step],
            recv_sem=strip_recv.at[which, place_of[axis]],
            device_id=device_along(axis, turned(place_of[axis], step)),
            device_id_type=MESH,
        )

    def send_strip(which):
        for step in range(1, parts):
            strip_copy(which, step).start()

    def take_strip(which, slot):
        pltpu.make_async_remote_copy(
            src_ref=own.at[which],
            dst_ref=strips.at[which, slot],
            send_sem=strip_send.at[which, 0],
            recv_sem=strip_recv.at[which, slot],
            device_id=device_along("row", col),
            device_id_type=MESH,
        ).wait_recv()

        def step(rows):
            wide[which, slot, rows, :] = strips[which, slot, rows, :].astype(jnp.float32)

        in_chunks(step)

    def sum_copy(which, tile):
        axis = SUM_AXIS[which]
        return pltpu.make_async_remote_copy(
            src_ref=partials.at[which, tile],
            dst_ref=sums.at[which, place_of[axis]],
            send_sem=sum_send.at[which, tile],
            recv_sem=sum_recv.at[which, place_of[axis]],
            device_id=device_along(axis, tile),
            device_id_type=MESH,
        )

    def send_sum(which, tile, totals):
        for a in range(side):
            partials[which, tile, a * side : (a + 1) * side, :] = totals[a].astype(jnp.bfloat16)

        @pl.when(tile != place_of[SUM_AXIS[which]])
        def _():
            sum_copy(which, tile).start()

    def added(which):
        place = place_of[SUM_AXIS[which]]
        for step in range(1, parts):
            slot = turned(place, -step)
            pltpu.make_async_remote_copy(
                src_ref=partials.at[which, 0],
                dst_ref=sums.at[which, slot],
                send_sem=sum_send.at[which, 0],
                recv_sem=sum_recv.at[which, slot],
                device_id=device_along("row", col),
                device_id_type=MESH,
            ).wait_recv()

        def read(rows):
            total = partials[which, place, rows, :].astype(jnp.float32)
            for step in range(1, parts):
                slot = turned(place, step)
                total = total + sums[which, slot, rows, :].astype(jnp.float32)
            return total

        return read

    def contract(totals, spread, spread_major, stream, stream_major):
        half = 8

        def run(index, totals):
            totals = list(totals)
            for inner in range(half):
                t = index * half + inner
                if stream_major:
                    block = stream[pl.ds(pl.multiple_of(t * side, side), side), :]
                else:
                    block = stream[pl.ds(t, side, stride=side), :]
                for a in range(side):
                    place = t * side + a if spread_major else a * side + t
                    totals[a] = totals[a] + spread[pl.ds(place, 1), :] * block
            return tuple(totals)

        return lax.fori_loop(0, side // half, run, totals)

    def zeros():
        return tuple(jnp.zeros((side, width), jnp.float32) for _ in range(side))

    def over_strip(which, step):
        place = place_of[STRIP_AXIS[which]]
        step(place, True)

        def run(index, carry):
            slot = turned(place, -index)
            take_strip(which, slot)
            step(slot, False)
            return carry

        lax.fori_loop(1, parts, run, 0)

    def put(target, totals):
        for a in range(side):
            target[a * side : (a + 1) * side, :] = totals[a]

    def grow(target, first, operands):
        totals = tuple(target[a * side : (a + 1) * side, :] for a in range(side))
        if first:
            totals = zeros()
        put(target, contract(totals, *operands))

    def norm_in(update, source):
        gain = gains_ref[update, 0:1, :]
        shift = shifts_ref[update, 0:1, :]

        def step(rows):
            inputs = source[rows, :].astype(jnp.float32)
            standard, inverse, normed = layer_norm(inputs, gain, shift)
            saved[update, STANDARD, rows, :] = standard
            inverses[update, 0, rows, :] = jnp.broadcast_to(inverse, standard.shape)
            cast[rows, :] = normed.astype(jnp.bfloat16)

        in_chunks(step)

    def project(update, start, stop):
        projected[:, start:stop] = matmul(cast[...], edge_weights_ref[update, :, start:stop])

    def edge(update, side_of, rows):
        start = 2 * side_of * width
        value = projected[rows, start : start + width]
        sigma = jax.nn.sigmoid(projected[rows, start + width : start + 2 * width])
        saved[update, VALUE_LEFT + 2 * side_of, rows, :] = value
        saved[update, SIGMA_LEFT + 2 * side_of, rows, :] = sigma
        return (sigma * value).astype(jnp.bfloat16)

    def gate_out(update, rows):
        gate = jax.nn.sigmoid(projected[rows, 4 * width :])
        saved[update, GATE, rows, :] = gate

    def pass_back(update):
        def step(rows):
            gated = upstream[rows, :] * saved[update, GATE, rows, :]
            cast[rows, :] = gated.astype(jnp.bfloat16)

        in_chunks(step)
        work[...] = matmul_transposed(cast[...], out_weights_ref[update])

    def product_back(update, which, rows, standard, inverse):
        grad = norm_backward(work[rows, :], standard, inverse, gains_ref[update, 1:2, :])
        grad = grad.astype(jnp.bfloat16)
        own[which, rows, :] = grad
        place = place_of[STRIP_AXIS[which]]
        wide[which, place, rows, :] = grad.astype(jnp.float32)

    def gate_piece(update, hidden):
        def step(rows):
            gate = saved[update, GATE, rows, :]
            term = upstream[rows, :] * hidden[rows, :] * gate * (1.0 - gate)
            pieces[rows, 4 * width :] = term.astype(jnp.bfloat16)

        in_chunks(step)

    def edge_pieces(update, side_of, rows, grad):
        value = saved[update, VALUE_LEFT + 2 * side_of, rows, :]
        sigma = saved[update, SIGMA_LEFT + 2 * side_of, rows, :]
        scaled = grad * sigma
        slope = scaled * value * (1.0 - sigma)
        start = 2 * side_of * width
        pieces[rows, start : start + width] = scaled.astype(jnp.bfloat16)
        pieces[rows, start + width : start + 2 * width] = slope.astype(jnp.bfloat16)
        edge_grads_ref[2 * update + side_of, rows, :] = grad.astype(jnp.bfloat16)

    def pieces_back(update, start, stop):
        return matmul_transposed(pieces[:, start:stop], edge_weights_ref[update, :, start:stop])

    def input_back(update, rows):
        return norm_backward(
            work[rows, :],
            saved[update, STANDARD, rows, :],
            inverses[update, 0, rows, :],
            gains_ref[update, 0:1, :],
        )

    for load in loads[:3]:
        load.wait()
    norm_in(0, pair_ref)
    loads[3].wait()
    project(0, 2 * width, 4 * width)

    def right_out_step(rows):
        right = edge(0, 1, rows)
        own[RIGHT_OUT, rows, :] = right
        wide[RIGHT_OUT, row, rows, :] = right.astype(jnp.float32)

    in_chunks(right_out_step)
    pl.semaphore_wait(barrier, 2 * (parts - 1))
    send_strip(RIGHT_OUT)
    project(0, 0, 2 * width)

    def left_out_step(rows):
        single[0, rows, :] = edge(0, 0, rows).astype(jnp.float32)

    in_chunks(left_out_step)

    def product_out_step(slot, first):
        totals = contract(zeros(), single.at[0], False, wide.at[RIGHT_OUT, slot], False)
        send_sum(PRODUCT_OUT, slot, totals)

    over_strip(RIGHT_OUT, product_out_step)
    project(0, 4 * width, 5 * width)
    loads[4].wait()
    loads[5].wait()

    def gate_step(rows):
        gate_out(0, rows)
        upstream[rows, :] = cotangent_ref[rows, :].astype(jnp.float32)

    in_chunks(gate_step)

    total_out = added(PRODUCT_OUT)

    def norm_out_step(rows):
        standard, inverse, normed = layer_norm(
            total_out(rows), gains_ref[0, 1:2, :], shifts_ref[0, 1:2, :]
        )
        saved[0, CENTRED, rows, :] = standard
        inverses[0, 1, rows, :] = jnp.broadcast_to(inverse, standard.shape)
        cast[rows, :] = normed.astype(jnp.bfloat16)

    in_chunks(norm_out_step)
    extra[0] = matmul(cast[...], out_weights_ref[0])

    def middle_step(rows):
        update = saved[0, GATE, rows, :] * extra[0, rows, :]
        middle[rows, :] = (pair_ref[rows, :].astype(jnp.float32) + update).astype(jnp.bfloat16)

    in_chunks(middle_step)

    norm_in(1, middle)
    project(1, 0, 2 * width)

    def left_in_step(rows):
        left = edge(1, 0, rows)
        own[LEFT_IN, rows, :] = left
        wide[LEFT_IN, col, rows, :] = left.astype(jnp.float32)

    in_chunks(left_in_step)
    send_strip(LEFT_IN)
    project(1, 2 * width, 5 * width)

    def right_in_step(rows):
        single[1, rows, :] = edge(1, 1, rows).astype(jnp.float32)

    in_chunks(right_in_step)

    def product_in_step(slot, first):
        totals = contract(zeros(), wide.at[LEFT_IN, slot], True, single.at[1], True)
        send_sum(PRODUCT_IN, slot, totals)

    over_strip(LEFT_IN, product_in_step)
    in_chunks(functools.partial(gate_out, 1))
    pass_back(1)

    total_in = added(PRODUCT_IN)

    def norm_in_step(rows):
        standard, inverse, normed = layer_norm(
            total_in(rows), gains_ref[1, 1:2, :], shifts_ref[1, 1:2, :]
        )
        cast[rows, :] = normed.astype(jnp.bfloat16)
        product_back(1, GRAD_IN, rows, standard, inverse)

    in_chunks(norm_in_step)
    send_strip(GRAD_IN)
    extra[1] = matmul(cast[...], out_weights_ref[1])
    gate_piece(1, extra.at[1])

    def left_in_back(slot, first):
        totals = contract(zeros(), single.at[1], False, wide.at[GRAD_IN, slot], False)
        send_sum(SUM_LEFT_IN, slot, totals)

    over_strip(GRAD_IN, left_in_back)
    for slot in range(parts):
        grow(
            grads,
            slot == 0,
            (wide.at[LEFT_IN, slot], False, wide.at[GRAD_IN, slot], True),
        )
    in_chunks(lambda rows: edge_pieces(1, 1, rows, grads[rows, :]))
    work[...] = pieces_back(1, 2 * width, 5 * width)
    sum_left_in = added(SUM_LEFT_IN)
    in_chunks(lambda rows: edge_pieces(1, 0, rows, sum_left_in(rows)))
    work[...] = work[...] + pieces_back(1, 0, 2 * width)

    def grad_middle_step(rows):
        upstream[rows, :] = upstream[rows, :] + input_back(1, rows)

    in_chunks(grad_middle_step)

    pass_back(0)

    def product_out_back(rows):
        product_back(0, GRAD_OUT, rows, saved[0, CENTRED, rows, :], inverses[0, 1, rows, :])

    in_chunks(product_out_back)
    send_strip(GRAD_OUT)
    gate_piece(0, extra.at[0])

    def right_out_back(slot, first):
        totals = contract(zeros(), wide.at[GRAD_OUT, slot], True, single.at[0], True)
        send_sum(SUM_RIGHT_OUT, slot, totals)

    over_strip(GRAD_OUT, right_out_back)
    for slot in range(parts):
        grow(
            grads,
            slot == 0,
            (wide.at[GRAD_OUT, slot], False, wide.at[RIGHT_OUT, slot], True),
        )
    in_chunks(lambda rows: edge_pieces(0, 0, rows, grads[rows, :]))
    work[...] = pieces_back(0, 0, 2 * width) + pieces_back(0, 4 * width, 5 * width)
    sum_right_out = added(SUM_RIGHT_OUT)
    in_chunks(lambda rows: edge_pieces(0, 1, rows, sum_right_out(rows)))
    work[...] = work[...] + pieces_back(0, 2 * width, 4 * width)

    def final_step(rows):
        total = upstream[rows, :] + input_back(0, rows)
        pair_grad_ref[rows, :] = total.astype(jnp.bfloat16)

    in_chunks(final_step)

    for which in range(4):
        for step in range(1, parts):
            strip_copy(which, step).wait_send()
            tile = turned(place_of[SUM_AXIS[which]], step)
            sum_copy(which, tile).wait_send()


def fused_body(pair, pair_cotangent, edge_weights, out_weights, norm_gains, norm_shifts):
    parts = lax.axis_size("row")
    side, _, width = pair.shape
    area = side * side
    tile = (area, width)
    arguments = (
        pair.reshape(tile),
        pair_cotangent.reshape(tile),
        edge_weights,
        out_weights,
        norm_gains,
        norm_shifts,
    )
    vmem = pl.BlockSpec(memory_space=pltpu.VMEM)
    semaphores = pltpu.SemaphoreType.DMA((4, parts))
    pair_grad, edge_grads = pl.pallas_call(
        functools.partial(kernel, parts, side),
        out_shape=(
            jax.ShapeDtypeStruct(tile, jnp.bfloat16),
            jax.ShapeDtypeStruct((4, *tile), jnp.bfloat16),
        ),
        in_specs=[pl.BlockSpec(memory_space=pltpu.HBM)] * 6,
        out_specs=(vmem, vmem),
        scratch_shapes=[
            *(pltpu.VMEM(argument.shape, argument.dtype) for argument in arguments),
            pltpu.VMEM((4, *tile), jnp.bfloat16),
            pltpu.VMEM((4, parts, *tile), jnp.bfloat16),
            pltpu.VMEM((4, parts, *tile), jnp.bfloat16),
            pltpu.VMEM((4, parts, *tile), jnp.bfloat16),
            pltpu.VMEM((4, parts, *tile), jnp.float32),
            pltpu.VMEM((2, *tile), jnp.float32),
            pltpu.VMEM((2, 7, *tile), jnp.float32),
            pltpu.VMEM((2, 2, *tile), jnp.float32),
            pltpu.VMEM((area, edge_weights.shape[2]), jnp.float32),
            pltpu.VMEM(tile, jnp.float32),
            pltpu.VMEM((2, *tile), jnp.float32),
            pltpu.VMEM(tile, jnp.float32),
            pltpu.VMEM(tile, jnp.bfloat16),
            pltpu.VMEM(tile, jnp.bfloat16),
            pltpu.VMEM(tile, jnp.float32),
            pltpu.VMEM((area, edge_weights.shape[2]), jnp.bfloat16),
            pltpu.SemaphoreType.DMA((len(arguments),)),
            semaphores,
            semaphores,
            semaphores,
            semaphores,
        ],
        compiler_params=pltpu.CompilerParams(
            collective_id=0, has_side_effects=True, vmem_limit_bytes=63 * 1024 * 1024
        ),
    )(*arguments)
    return pair_grad.reshape(pair.shape), edge_grads.reshape(4, *pair.shape)


def body(pair, pair_cotangent, edge_weights, out_weights, norm_gains, norm_shifts):
    arguments = (pair, pair_cotangent, edge_weights, out_weights, norm_gains, norm_shifts)
    square = lax.axis_size("row") == lax.axis_size("col") and pair.shape[0] == pair.shape[1]
    if square and pair.shape[0] % 16 == 0:
        return fused_body(*arguments)
    return gathered_body(*arguments)


def solution(mesh):
    return jax.shard_map(
        body,
        mesh=mesh,
        in_specs=(
            P(("groups", "row"), "col", None),
            P(("groups", "row"), "col", None),
            P(),
            P(),
            P(),
            P(),
        ),
        out_specs=(P(("groups", "row"), "col", None), P(None, ("groups", "row"), "col", None)),
        check_vma=False,
    )
```

```python
import functools

import jax
import jax.numpy as jnp
from jax import lax
from jax.experimental import pallas as pl
from jax.experimental.pallas import tpu as pltpu
from jax.sharding import PartitionSpec as P

EPSILON = 1e-05


def product_of(form, left, right):
    return jnp.einsum(form, left, right, preferred_element_type=jnp.float32)


def layer_norm(inputs, norm_gain, norm_shift):
    centre = jnp.mean(inputs, axis=-1, keepdims=True)
    centred = inputs - centre
    inverse = lax.rsqrt(jnp.mean(centred * centred, axis=-1, keepdims=True) + EPSILON)
    standard = centred * inverse
    return (standard, inverse, standard * norm_gain + norm_shift)


def norm_backward(upstream, standard, inverse, norm_gain):
    scaled = upstream * norm_gain
    mean_grad = jnp.mean(scaled, axis=-1, keepdims=True)
    second = jnp.mean(scaled * standard, axis=-1, keepdims=True)
    return (scaled - mean_grad - standard * second) * inverse


def edges_forward(inputs, weights, norm_gain, norm_shift):
    standard, inverse, normed = layer_norm(inputs, norm_gain, norm_shift)
    projected = product_of("ijc,cd->ijd", normed.astype(jnp.bfloat16), weights)
    width = weights.shape[1] // 5
    value_left = projected[..., :width]
    sigma_left = jax.nn.sigmoid(projected[..., width : 2 * width])
    value_right = projected[..., 2 * width : 3 * width]
    sigma_right = jax.nn.sigmoid(projected[..., 3 * width : 4 * width])
    out_gate = jax.nn.sigmoid(projected[..., 4 * width :])
    left_edge = (sigma_left * value_left).astype(jnp.bfloat16)
    right_edge = (sigma_right * value_right).astype(jnp.bfloat16)
    saved = (standard, inverse, value_left, sigma_left, value_right, sigma_right, out_gate)
    return (left_edge, right_edge, saved)


def output_forward(product, out_weight, norm_gain, norm_shift):
    standard, inverse, normed = layer_norm(product, norm_gain, norm_shift)
    hidden_out = product_of("ijd,dc->ijc", normed.astype(jnp.bfloat16), out_weight)
    return (hidden_out, standard, inverse)


def output_backward(upstream, out_weight, norm_gain, out_gate, stats):
    hidden_out, standard, inverse = stats
    grad_hidden = (upstream * out_gate).astype(jnp.bfloat16)
    gate_term = upstream * hidden_out * out_gate * (1.0 - out_gate)
    grad_normed = product_of("ijc,dc->ijd", grad_hidden, out_weight)
    grad_product = norm_backward(grad_normed, standard, inverse, norm_gain).astype(jnp.bfloat16)
    return (grad_product, gate_term)


def edges_backward(grad_left, grad_right, gate_term, weights, norm_gain, saved):
    standard, inverse, value_left, sigma_left, value_right, sigma_right, out_gate = saved
    pieces = jnp.concatenate(
        [
            grad_left * sigma_left,
            grad_left * value_left * sigma_left * (1.0 - sigma_left),
            grad_right * sigma_right,
            grad_right * value_right * sigma_right * (1.0 - sigma_right),
            gate_term,
        ],
        axis=-1,
    )
    grad_normed = product_of("ijd,cd->ijc", pieces.astype(jnp.bfloat16), weights)
    return norm_backward(grad_normed, standard, inverse, norm_gain)


def row_strip(tile):
    return lax.all_gather(tile, "col", axis=1, tiled=True)


def column_strip(tile):
    return lax.all_gather(tile, "row", axis=0, tiled=True)


def shuffle_rows(tile):
    return lax.all_to_all(tile, "row", split_axis=1, concat_axis=0, tiled=True)


def shuffle_columns(tile):
    return lax.all_to_all(tile, "col", split_axis=0, concat_axis=1, tiled=True)


def transposed_columns(tile):
    row_devices = lax.axis_size("row")
    column_devices = lax.axis_size("col")
    moved = shuffle_columns(shuffle_rows(tile))
    gathered = column_strip(jnp.swapaxes(moved, 0, 1))
    total = gathered.shape[0]
    block = total // (row_devices * column_devices)
    gathered = gathered.reshape(
        row_devices, column_devices, block, gathered.shape[1], gathered.shape[2]
    )
    return jnp.swapaxes(gathered, 0, 1).reshape(total, gathered.shape[3], gathered.shape[4])


def transposed_rows(tile):
    row_devices = lax.axis_size("row")
    column_devices = lax.axis_size("col")
    moved = shuffle_rows(shuffle_columns(tile))
    gathered = row_strip(jnp.swapaxes(moved, 0, 1))
    total = gathered.shape[1]
    block = total // (row_devices * column_devices)
    gathered = gathered.reshape(
        gathered.shape[0], column_devices, row_devices, block, gathered.shape[2]
    )
    return jnp.swapaxes(gathered, 1, 2).reshape(gathered.shape[0], total, gathered.shape[4])


def gathered_body(pair, pair_cotangent, edge_weights, out_weights, norm_gains, norm_shifts):
    pair_float = pair.astype(jnp.float32)
    left_out, right_out, saved_out = edges_forward(
        pair_float, edge_weights[0], norm_gains[0, 0], norm_shifts[0, 0]
    )
    strip_right = column_strip(right_out)
    product_out = product_of("ikc,kjc->ijc", row_strip(left_out), transposed_columns(right_out))
    stats_out = output_forward(product_out, out_weights[0], norm_gains[0, 1], norm_shifts[0, 1])
    middle = (pair_float + saved_out[6] * stats_out[0]).astype(jnp.bfloat16)
    left_in, right_in, saved_in = edges_forward(
        middle.astype(jnp.float32), edge_weights[1], norm_gains[1, 0], norm_shifts[1, 0]
    )
    product_in = product_of("ikc,kjc->ijc", transposed_rows(left_in), column_strip(right_in))
    stats_in = output_forward(product_in, out_weights[1], norm_gains[1, 1], norm_shifts[1, 1])
    upstream = pair_cotangent.astype(jnp.float32)
    grad_product_in, gate_in = output_backward(
        upstream, out_weights[1], norm_gains[1, 1], saved_in[6], stats_in
    )
    grad_left_in = product_of(
        "kjc,jic->kic", row_strip(right_in), transposed_columns(grad_product_in)
    )
    grad_right_in = product_of("kic,ijc->kjc", row_strip(left_in), column_strip(grad_product_in))
    grad_middle = upstream + edges_backward(
        grad_left_in, grad_right_in, gate_in, edge_weights[1], norm_gains[1, 0], saved_in
    )
    grad_product_out, gate_outer = output_backward(
        grad_middle, out_weights[0], norm_gains[0, 1], saved_out[6], stats_out
    )
    grad_left_out = product_of("ijc,jkc->ikc", row_strip(grad_product_out), strip_right)
    grad_right_out = product_of(
        "jic,ikc->jkc", transposed_rows(grad_product_out), column_strip(left_out)
    )
    pair_grad = grad_middle + edges_backward(
        grad_left_out, grad_right_out, gate_outer, edge_weights[0], norm_gains[0, 0], saved_out
    )
    edge_grads = jnp.stack([grad_left_out, grad_right_out, grad_left_in, grad_right_in])
    return (pair_grad.astype(jnp.bfloat16), edge_grads.astype(jnp.bfloat16))


MESH = pl.DeviceIdType.MESH
RIGHT_OUT, LEFT_IN, GRAD_IN, GRAD_OUT = range(4)
PRODUCT_OUT, PRODUCT_IN, SUM_LEFT_IN, SUM_RIGHT_OUT = range(4)
STRIP_AXIS = ("col", "row", "col", "row")
SUM_AXIS = ("row", "col", "row", "col")
STANDARD, VALUE_LEFT, SIGMA_LEFT, VALUE_RIGHT, SIGMA_RIGHT, GATE, CENTRED = range(7)


def matmul(left, right):
    return jnp.dot(left, right, preferred_element_type=jnp.float32)


def matmul_transposed(left, right):
    return lax.dot_general(
        left, right, (((1,), (1,)), ((), ())), preferred_element_type=jnp.float32
    )


def kernel(
    parts,
    side,
    pair_hbm,
    cotangent_hbm,
    edge_weights_hbm,
    out_weights_hbm,
    gains_hbm,
    shifts_hbm,
    pair_grad_hbm,
    edge_grads_hbm,
    pair_grad_ref,
    edge_grads_ref,
    pair_ref,
    cotangent_ref,
    edge_weights_ref,
    out_weights_ref,
    gains_ref,
    shifts_ref,
    own,
    strips,
    partials,
    sums,
    wide,
    single,
    saved,
    inverses,
    projected,
    work,
    extra,
    grads,
    middle,
    cast,
    upstream,
    pieces,
    load_sem,
    store_sem,
    strip_send,
    strip_recv,
    sum_send,
    sum_recv,
):
    row = lax.axis_index("row")
    col = lax.axis_index("col")
    area = side * side
    width = pair_ref.shape[1]
    chunk = min(area, 128)
    place_of = {"row": col, "col": row}

    def turned(index, step):
        return lax.rem(index + parts + step, parts)

    def device_along(axis, place):
        return {"row": row, "col": place} if axis == "row" else {"row": place, "col": col}

    barrier = pltpu.get_barrier_semaphore()
    for axis in ("row", "col"):
        for step in range(1, parts):
            pl.semaphore_signal(
                barrier,
                inc=1,
                device_id=device_along(axis, turned(place_of[axis], step)),
                device_id_type=MESH,
            )

    loads = [
        pltpu.make_async_copy(source, target, load_sem.at[index])
        for index, (source, target) in enumerate(
            (
                (pair_hbm, pair_ref),
                (gains_hbm, gains_ref),
                (shifts_hbm, shifts_ref),
                (edge_weights_hbm, edge_weights_ref),
                (out_weights_hbm, out_weights_ref),
                (cotangent_hbm, cotangent_ref),
            )
        )
    ]
    for load in loads:
        load.start()
    stores = [
        pltpu.make_async_copy(edge_grads_ref.at[index], edge_grads_hbm.at[index], store_sem.at[index])
        for index in range(4)
    ]
    stores.append(pltpu.make_async_copy(pair_grad_ref, pair_grad_hbm, store_sem.at[4]))

    def in_chunks(step):
        for start in range(0, area, chunk):
            step(pl.ds(start, chunk))

    def strip_copy(which, step):
        axis = STRIP_AXIS[which]
        return pltpu.make_async_remote_copy(
            src_ref=own.at[which],
            dst_ref=strips.at[which, place_of[axis]],
            send_sem=strip_send.at[which, step],
            recv_sem=strip_recv.at[which, place_of[axis]],
            device_id=device_along(axis, turned(place_of[axis], step)),
            device_id_type=MESH,
        )

    def send_strip(which):
        for step in range(1, parts):
            strip_copy(which, step).start()

    def take_strip(which, slot):
        pltpu.make_async_remote_copy(
            src_ref=own.at[which],
            dst_ref=strips.at[which, slot],
            send_sem=strip_send.at[which, 0],
            recv_sem=strip_recv.at[which, slot],
            device_id=device_along("row", col),
            device_id_type=MESH,
        ).wait_recv()

        def step(rows):
            wide[which, slot, rows, :] = strips[which, slot, rows, :].astype(jnp.float32)

        in_chunks(step)

    def sum_copy(which, tile):
        axis = SUM_AXIS[which]
        return pltpu.make_async_remote_copy(
            src_ref=partials.at[which, tile],
            dst_ref=sums.at[which, place_of[axis]],
            send_sem=sum_send.at[which, tile],
            recv_sem=sum_recv.at[which, place_of[axis]],
            device_id=device_along(axis, tile),
            device_id_type=MESH,
        )

    def send_sum(which, tile, totals):
        for a in range(side):
            partials[which, tile, a * side : (a + 1) * side, :] = totals[a].astype(jnp.bfloat16)

        @pl.when(tile != place_of[SUM_AXIS[which]])
        def _():
            sum_copy(which, tile).start()

    def added(which):
        place = place_of[SUM_AXIS[which]]
        for step in range(1, parts):
            slot = turned(place, -step)
            pltpu.make_async_remote_copy(
                src_ref=partials.at[which, 0],
                dst_ref=sums.at[which, slot],
                send_sem=sum_send.at[which, 0],
                recv_sem=sum_recv.at[which, slot],
                device_id=device_along("row", col),
                device_id_type=MESH,
            ).wait_recv()

        def read(rows):
            total = partials[which, place, rows, :].astype(jnp.float32)
            for step in range(1, parts):
                slot = turned(place, step)
                total = total + sums[which, slot, rows, :].astype(jnp.float32)
            return total

        return read

    def contract(totals, spread, spread_major, stream, stream_major):
        half = 8

        def run(index, totals):
            totals = list(totals)
            for inner in range(half):
                t = index * half + inner
                if stream_major:
                    block = stream[pl.ds(pl.multiple_of(t * side, side), side), :]
                else:
                    block = stream[pl.ds(t, side, stride=side), :]
                for a in range(side):
                    place = t * side + a if spread_major else a * side + t
                    totals[a] = totals[a] + spread[pl.ds(place, 1), :] * block
            return tuple(totals)

        return lax.fori_loop(0, side // half, run, totals)

    def zeros():
        return tuple(jnp.zeros((side, width), jnp.float32) for _ in range(side))

    def over_strip(which, step):
        place = place_of[STRIP_AXIS[which]]
        step(place, True)

        def run(index, carry):
            slot = turned(place, -index)
            take_strip(which, slot)
            step(slot, False)
            return carry

        lax.fori_loop(1, parts, run, 0)

    def put(target, totals):
        for a in range(side):
            target[a * side : (a + 1) * side, :] = totals[a]

    def grow(target, first, operands):
        totals = tuple(target[a * side : (a + 1) * side, :] for a in range(side))
        if first:
            totals = zeros()
        put(target, contract(totals, *operands))

    def norm_in(update, source):
        gain = gains_ref[update, 0:1, :]
        shift = shifts_ref[update, 0:1, :]

        def step(rows):
            inputs = source[rows, :].astype(jnp.float32)
            standard, inverse, normed = layer_norm(inputs, gain, shift)
            saved[update, STANDARD, rows, :] = standard
            inverses[update, 0, rows, :] = jnp.broadcast_to(inverse, standard.shape)
            cast[rows, :] = normed.astype(jnp.bfloat16)

        in_chunks(step)

    def project(update, start, stop):
        projected[:, start:stop] = matmul(cast[...], edge_weights_ref[update, :, start:stop])

    def edge(update, side_of, rows):
        start = 2 * side_of * width
        value = projected[rows, start : start + width]
        sigma = jax.nn.sigmoid(projected[rows, start + width : start + 2 * width])
        saved[update, VALUE_LEFT + 2 * side_of, rows, :] = value
        saved[update, SIGMA_LEFT + 2 * side_of, rows, :] = sigma
        return (sigma * value).astype(jnp.bfloat16)

    def gate_out(update, rows):
        gate = jax.nn.sigmoid(projected[rows, 4 * width :])
        saved[update, GATE, rows, :] = gate

    def pass_back(update):
        def step(rows):
            gated = upstream[rows, :] * saved[update, GATE, rows, :]
            cast[rows, :] = gated.astype(jnp.bfloat16)

        in_chunks(step)
        work[...] = matmul_transposed(cast[...], out_weights_ref[update])

    def product_back(update, which, rows, standard, inverse):
        grad = norm_backward(work[rows, :], standard, inverse, gains_ref[update, 1:2, :])
        grad = grad.astype(jnp.bfloat16)
        own[which, rows, :] = grad
        place = place_of[STRIP_AXIS[which]]
        wide[which, place, rows, :] = grad.astype(jnp.float32)

    def gate_piece(update, hidden):
        def step(rows):
            gate = saved[update, GATE, rows, :]
            term = upstream[rows, :] * hidden[rows, :] * gate * (1.0 - gate)
            pieces[rows, 4 * width :] = term.astype(jnp.bfloat16)

        in_chunks(step)

    def edge_pieces(update, side_of, rows, grad):
        value = saved[update, VALUE_LEFT + 2 * side_of, rows, :]
        sigma = saved[update, SIGMA_LEFT + 2 * side_of, rows, :]
        scaled = grad * sigma
        slope = scaled * value * (1.0 - sigma)
        start = 2 * side_of * width
        pieces[rows, start : start + width] = scaled.astype(jnp.bfloat16)
        pieces[rows, start + width : start + 2 * width] = slope.astype(jnp.bfloat16)
        edge_grads_ref[2 * update + side_of, rows, :] = grad.astype(jnp.bfloat16)

    def pieces_back(update, start, stop):
        return matmul_transposed(pieces[:, start:stop], edge_weights_ref[update, :, start:stop])

    def input_back(update, rows):
        return norm_backward(
            work[rows, :],
            saved[update, STANDARD, rows, :],
            inverses[update, 0, rows, :],
            gains_ref[update, 0:1, :],
        )

    for load in loads[:3]:
        load.wait()
    norm_in(0, pair_ref)
    loads[3].wait()
    project(0, 2 * width, 4 * width)

    def right_out_step(rows):
        right = edge(0, 1, rows)
        own[RIGHT_OUT, rows, :] = right
        wide[RIGHT_OUT, row, rows, :] = right.astype(jnp.float32)

    in_chunks(right_out_step)
    pl.semaphore_wait(barrier, 2 * (parts - 1))
    send_strip(RIGHT_OUT)
    project(0, 0, 2 * width)

    def left_out_step(rows):
        single[0, rows, :] = edge(0, 0, rows).astype(jnp.float32)

    in_chunks(left_out_step)

    def product_out_step(slot, first):
        totals = contract(zeros(), single.at[0], False, wide.at[RIGHT_OUT, slot], False)
        send_sum(PRODUCT_OUT, slot, totals)

    over_strip(RIGHT_OUT, product_out_step)
    project(0, 4 * width, 5 * width)
    loads[4].wait()
    loads[5].wait()

    def gate_step(rows):
        gate_out(0, rows)
        upstream[rows, :] = cotangent_ref[rows, :].astype(jnp.float32)

    in_chunks(gate_step)

    total_out = added(PRODUCT_OUT)

    def norm_out_step(rows):
        standard, inverse, normed = layer_norm(
            total_out(rows), gains_ref[0, 1:2, :], shifts_ref[0, 1:2, :]
        )
        saved[0, CENTRED, rows, :] = standard
        inverses[0, 1, rows, :] = jnp.broadcast_to(inverse, standard.shape)
        cast[rows, :] = normed.astype(jnp.bfloat16)

    in_chunks(norm_out_step)
    extra[0] = matmul(cast[...], out_weights_ref[0])

    def middle_step(rows):
        update = saved[0, GATE, rows, :] * extra[0, rows, :]
        middle[rows, :] = (pair_ref[rows, :].astype(jnp.float32) + update).astype(jnp.bfloat16)

    in_chunks(middle_step)

    norm_in(1, middle)
    project(1, 0, 2 * width)

    def left_in_step(rows):
        left = edge(1, 0, rows)
        own[LEFT_IN, rows, :] = left
        wide[LEFT_IN, col, rows, :] = left.astype(jnp.float32)

    in_chunks(left_in_step)
    send_strip(LEFT_IN)
    project(1, 2 * width, 5 * width)

    def right_in_step(rows):
        single[1, rows, :] = edge(1, 1, rows).astype(jnp.float32)

    in_chunks(right_in_step)

    def product_in_step(slot, first):
        totals = contract(zeros(), wide.at[LEFT_IN, slot], True, single.at[1], True)
        send_sum(PRODUCT_IN, slot, totals)

    over_strip(LEFT_IN, product_in_step)
    in_chunks(functools.partial(gate_out, 1))
    pass_back(1)

    total_in = added(PRODUCT_IN)

    def norm_in_step(rows):
        standard, inverse, normed = layer_norm(
            total_in(rows), gains_ref[1, 1:2, :], shifts_ref[1, 1:2, :]
        )
        cast[rows, :] = normed.astype(jnp.bfloat16)
        product_back(1, GRAD_IN, rows, standard, inverse)

    in_chunks(norm_in_step)
    send_strip(GRAD_IN)
    extra[1] = matmul(cast[...], out_weights_ref[1])
    gate_piece(1, extra.at[1])

    def left_in_back(slot, first):
        totals = contract(zeros(), single.at[1], False, wide.at[GRAD_IN, slot], False)
        send_sum(SUM_LEFT_IN, slot, totals)

    over_strip(GRAD_IN, left_in_back)
    for slot in range(parts):
        grow(
            grads,
            slot == 0,
            (wide.at[LEFT_IN, slot], False, wide.at[GRAD_IN, slot], True),
        )
    in_chunks(lambda rows: edge_pieces(1, 1, rows, grads[rows, :]))
    work[...] = pieces_back(1, 2 * width, 5 * width)
    sum_left_in = added(SUM_LEFT_IN)
    in_chunks(lambda rows: edge_pieces(1, 0, rows, sum_left_in(rows)))
    work[...] = work[...] + pieces_back(1, 0, 2 * width)

    stores[2].start()
    stores[3].start()

    def grad_middle_step(rows):
        upstream[rows, :] = upstream[rows, :] + input_back(1, rows)

    in_chunks(grad_middle_step)

    pass_back(0)

    def product_out_back(rows):
        product_back(0, GRAD_OUT, rows, saved[0, CENTRED, rows, :], inverses[0, 1, rows, :])

    in_chunks(product_out_back)
    send_strip(GRAD_OUT)
    gate_piece(0, extra.at[0])

    def right_out_back(slot, first):
        totals = contract(zeros(), wide.at[GRAD_OUT, slot], True, single.at[0], True)
        send_sum(SUM_RIGHT_OUT, slot, totals)

    over_strip(GRAD_OUT, right_out_back)
    for slot in range(parts):
        grow(
            grads,
            slot == 0,
            (wide.at[GRAD_OUT, slot], False, wide.at[RIGHT_OUT, slot], True),
        )
    in_chunks(lambda rows: edge_pieces(0, 0, rows, grads[rows, :]))
    work[...] = pieces_back(0, 0, 2 * width) + pieces_back(0, 4 * width, 5 * width)
    sum_right_out = added(SUM_RIGHT_OUT)
    in_chunks(lambda rows: edge_pieces(0, 1, rows, sum_right_out(rows)))
    work[...] = work[...] + pieces_back(0, 2 * width, 4 * width)

    stores[0].start()
    stores[1].start()

    def final_step(rows):
        total = upstream[rows, :] + input_back(0, rows)
        pair_grad_ref[rows, :] = total.astype(jnp.bfloat16)

    in_chunks(final_step)
    stores[4].start()
    for store in stores:
        store.wait()

    for which in range(4):
        for step in range(1, parts):
            strip_copy(which, step).wait_send()
            tile = turned(place_of[SUM_AXIS[which]], step)
            sum_copy(which, tile).wait_send()


def fused_body(pair, pair_cotangent, edge_weights, out_weights, norm_gains, norm_shifts):
    parts = lax.axis_size("row")
    side, _, width = pair.shape
    area = side * side
    tile = (area, width)
    arguments = (
        pair.reshape(tile),
        pair_cotangent.reshape(tile),
        edge_weights,
        out_weights,
        norm_gains,
        norm_shifts,
    )
    hbm = pl.BlockSpec(memory_space=pltpu.HBM)
    semaphores = pltpu.SemaphoreType.DMA((4, parts))
    pair_grad, edge_grads = pl.pallas_call(
        functools.partial(kernel, parts, side),
        out_shape=(
            jax.ShapeDtypeStruct(tile, jnp.bfloat16),
            jax.ShapeDtypeStruct((4, *tile), jnp.bfloat16),
        ),
        in_specs=[hbm] * 6,
        out_specs=(hbm, hbm),
        scratch_shapes=[
            pltpu.VMEM(tile, jnp.bfloat16),
            pltpu.VMEM((4, *tile), jnp.bfloat16),
            *(pltpu.VMEM(argument.shape, argument.dtype) for argument in arguments),
            pltpu.VMEM((4, *tile), jnp.bfloat16),
            pltpu.VMEM((4, parts, *tile), jnp.bfloat16),
            pltpu.VMEM((4, parts, *tile), jnp.bfloat16),
            pltpu.VMEM((4, parts, *tile), jnp.bfloat16),
            pltpu.VMEM((4, parts, *tile), jnp.float32),
            pltpu.VMEM((2, *tile), jnp.float32),
            pltpu.VMEM((2, 7, *tile), jnp.float32),
            pltpu.VMEM((2, 2, *tile), jnp.float32),
            pltpu.VMEM((area, edge_weights.shape[2]), jnp.float32),
            pltpu.VMEM(tile, jnp.float32),
            pltpu.VMEM((2, *tile), jnp.float32),
            pltpu.VMEM(tile, jnp.float32),
            pltpu.VMEM(tile, jnp.bfloat16),
            pltpu.VMEM(tile, jnp.bfloat16),
            pltpu.VMEM(tile, jnp.float32),
            pltpu.VMEM((area, edge_weights.shape[2]), jnp.bfloat16),
            pltpu.SemaphoreType.DMA((len(arguments),)),
            pltpu.SemaphoreType.DMA((5,)),
            semaphores,
            semaphores,
            semaphores,
            semaphores,
        ],
        compiler_params=pltpu.CompilerParams(
            collective_id=0, has_side_effects=True, vmem_limit_bytes=63 * 1024 * 1024
        ),
    )(*arguments)
    return pair_grad.reshape(pair.shape), edge_grads.reshape(4, *pair.shape)


def body(pair, pair_cotangent, edge_weights, out_weights, norm_gains, norm_shifts):
    arguments = (pair, pair_cotangent, edge_weights, out_weights, norm_gains, norm_shifts)
    square = lax.axis_size("row") == lax.axis_size("col") and pair.shape[0] == pair.shape[1]
    if square and pair.shape[0] % 16 == 0:
        return fused_body(*arguments)
    return gathered_body(*arguments)


def solution(mesh):
    return jax.shard_map(
        body,
        mesh=mesh,
        in_specs=(
            P(("groups", "row"), "col", None),
            P(("groups", "row"), "col", None),
            P(),
            P(),
            P(),
            P(),
        ),
        out_specs=(P(("groups", "row"), "col", None), P(None, ("groups", "row"), "col", None)),
        check_vma=False,
    )
```
